256 devices in a mesh: clip: 4 (over y), band: 4 (over x_hi, core), chan: 16 (over x_lo, z).
Axes of the slice: x: 4 (x_hi: 2, x_lo: 2; x = x_hi * 2 + x_lo), y: 4, z: 8, core: 2. Of those that a mesh axis runs over, the one named last changes fastest.
Arguments:
- frames: bfloat16 [512, 4, 40960], P(None, 'clip', ('band', 'chan')), may hold values from -6 to 6
- weight: bfloat16 [512, 3, 3, 512], P('chan'), may hold values from -0.09375 to 0.09375
- bias: float32 [512], replicated, may hold values from -3 to 3
- cotangent: bfloat16 [512, 4, 40960], P(None, 'clip', ('band', 'chan')), may hold values from -6 to 6
Outputs:
- outputs: bfloat16 [512, 4, 40960], P(None, 'clip', ('band', 'chan'))
- grad_frames: bfloat16 [512, 4, 40960], P(None, 'clip', ('band', 'chan'))
- grad_weight: float32 [512, 3, 3, 512], P('chan')
- grad_bias: float32 [512], P('chan')
The draws below stay inside these ranges and needn't reach their ends.
All inputs are finite; a program needn't handle non-finite values.
Results may differ from the reference program's by a relative error of at most 0.001.
Values may be sent and summed in bfloat16 or wider, within the bound.
No kernel may reach another device: no remote copies, remote signals or barrier semaphores. Data moves between devices by JAX's collectives and lax.ppermute only.
A program may use at most 128 MiB of HBM per device.

```python
import math
import jax
import jax.numpy as jnp
from jax import lax

C = 512
W = 160
H = 256
FRAMES = 4


def block_scale(stream_key, dims, cuts, smallest, top_value):
    gain = 1.0
    for dim, parts in cuts:
        steps = jax.random.uniform(jax.random.fold_in(jax.random.fold_in(stream_key, 6), dim), (parts,), jnp.float32, smallest / len(cuts), top_value / len(cuts))
        gain = gain * jnp.repeat(jnp.exp(steps), dims[dim] // parts).reshape((-1,) + (1,) * (len(dims) - 1 - dim))
    return gain


def normal_values(stream_key, dims, deviation, limit, shards=(), kind=jnp.bfloat16):
    values = deviation * jax.random.normal(stream_key, dims, jnp.float32)
    if shards:
        values = values * block_scale(stream_key, dims, shards, -0.22, 0.18)
    return jnp.clip(values, -limit, limit).astype(kind)


def setup_inputs(seed: int = 0) -> dict:
    splits = jax.random.split(jax.random.key(seed), 5)
    return {
        "frames": normal_values(splits[0], (C, FRAMES, H * W), 1.0, 6.0, ((1, 4), (2, 64))),
        "weight": normal_values(splits[1], (C, 3, 3, C), (9 * C) ** -0.5, 0.09375, ((0, 16),)),
        "bias": normal_values(splits[2], (C,), 0.5, 3.0, (), jnp.float32),
        "cotangent": normal_values(splits[3], (C, FRAMES, H * W), 1.0, 6.0, ((1, 4), (2, 64))),
    }


def reference(frames, weight, bias, cotangent):
    channels, frame_count, cell_total = frames.shape
    row_count = cell_total // W
    inputs = frames.astype(jnp.float32).reshape(channels, frame_count, row_count, W)
    kernel = weight.astype(jnp.float32)
    upstream = cotangent.astype(jnp.float32).reshape(channels, frame_count, row_count, W)
    margin = ((0, 0), (0, 0), (1, 1), (1, 1))
    padded_in = jnp.pad(inputs, margin)
    padded_cot = jnp.pad(upstream, margin)
    scale = 1.0 / math.sqrt(frame_count * row_count * W)
    running = jnp.zeros(inputs.shape, jnp.float32) + bias[:, None, None, None]
    grad_in = jnp.zeros(inputs.shape, jnp.float32)
    tap_rows = []
    for a in range(3):
        tap_row = []
        for b in range(3):
            window = padded_in[:, :, a:a + row_count, b:b + W]
            running = running + jnp.einsum('ifhw,oi->ofhw', window, kernel[:, a, b, :])
            back = padded_cot[:, :, 2 - a:2 - a + row_count, 2 - b:2 - b + W]
            grad_in = grad_in + jnp.einsum('ofhw,oi->ifhw', back, kernel[:, a, b, :])
            tap_row.append(jnp.einsum('ifhw,ofhw->oi', window, upstream))
        tap_rows.append(jnp.stack(tap_row, axis=1))
    grad_weight = jnp.stack(tap_rows, axis=1) * scale
    grad_bias = lax.optimization_barrier(jnp.sum(upstream, axis=(1, 2, 3))) * scale
    outputs = running.reshape(channels, frame_count, cell_total).astype(jnp.bfloat16)
    grad_frames = grad_in.reshape(channels, frame_count, cell_total).astype(jnp.bfloat16)
    return (outputs, grad_frames, grad_weight, grad_bias)
```

```python
import functools
import math

import jax
import jax.numpy as jnp
from jax import lax
from jax.experimental import pallas as pl
from jax.experimental.pallas import tpu as pltpu
from jax.sharding import Mesh, PartitionSpec as P

C = 512
HALF = 256
W = 160
S = 640
TAPS = 9
AXES = ("y", "xh", "core", "xl", "z")
SIZES = (4, 2, 2, 2, 8)
CELLS = ("xh", "core", "xl", "z")
ROWS = 80
VMEM = 56 * 1024 * 1024

bf16 = jnp.bfloat16
f16 = jnp.float16
f32 = jnp.float32


def vmem():
    return pl.BlockSpec(memory_space=pltpu.VMEM)


def smem():
    return pl.BlockSpec(memory_space=pltpu.SMEM)


def params():
    return pltpu.CompilerParams(vmem_limit_bytes=VMEM)


def roll(x, shift):
    return pltpu.roll(x, shift % x.shape[-1], x.ndim - 1)


def pack_row(wide, tile, start):
    lane = lax.broadcasted_iota(jnp.int32, (128, 128), 1)
    tile = tile.astype(f32)
    total = jnp.zeros((128, 128), f32)
    for g in range(4):
        part = roll(tile[128 * g:128 * (g + 1)], 32 * g - start)
        total = jnp.where((lane >= 32 * g) & (lane < 32 * g + 32), part, total)
    return jnp.concatenate([wide, total.astype(bf16)], axis=0)


def pack_kernel(core_ref, f_ref, g_ref, fl_ref, ff_ref, gl_ref, gf_ref, swap_ref):
    for x, last, first in ((f_ref, fl_ref, ff_ref), (g_ref, gl_ref, gf_ref)):
        last[...] = pack_row(x[:, 512:640], x[:, 384:512], 96)
        first[...] = pack_row(x[:, 0:128], x[:, 128:256], 0)
    other = pl.multiple_of((1 - core_ref[0]) * HALF, HALF)
    swap_ref[:HALF, :] = f_ref[pl.ds(other, HALF), :]
    swap_ref[HALF:, :] = g_ref[...]


def pack(core, f, g):
    row = jax.ShapeDtypeStruct((640, 128), bf16)
    return pl.pallas_call(
        pack_kernel,
        out_shape=(row, row, row, row, jax.ShapeDtypeStruct((HALF + C, S), bf16)),
        in_specs=[smem(), vmem(), vmem()],
        out_specs=(vmem(),) * 5,
        compiler_params=params(),
        name="pack",
    )(core, f, g)


def column_masks(rows):
    column = lax.broadcasted_iota(jnp.int32, (rows, S), 1) % W
    return column != 0, None, column != W - 1


def fill(ext, rows, cells, before, after, groups):
    ext[:rows, 256:896] = cells
    ext[:rows, 128:256] = before[0]
    ext[:rows, 896:1024] = after[0]
    tail_before = before[1].astype(f32)
    tail_after = after[1].astype(f32)
    for k, g in enumerate(groups):
        ext[128 * k:128 * (k + 1), 0:128] = pltpu.roll(tail_before, (96 - 32 * g) % 128, 1).astype(bf16)
        ext[128 * k:128 * (k + 1), 1024:1152] = pltpu.roll(tail_after, (128 - 32 * g) % 128, 1).astype(bf16)


def window(ext, rows, da, db, masks):
    start = 256 + da * W + db
    x = ext[pl.ds(rows[0], rows[1]), :][:, start:start + S]
    mask = masks[db + 1]
    if mask is not None:
        x = jnp.where(mask, x, jnp.zeros_like(x))
    return x


def dw_kernel(core_ref, f_ref, g_ref, before_ref, after_ref, swap_ref, halo_ref, out_ref, peak_ref, ext, win, cot):
    core = core_ref[0]
    mine = pl.multiple_of(core * HALF, HALF)
    masks = column_masks(HALF)
    groups = (2 * core, 2 * core + 1)
    cot[:, :S] = g_ref[...]
    cot[:, S:] = swap_ref[HALF:, :]
    for seg in range(2):
        if seg == 0:
            cells = f_ref[pl.ds(mine, HALF), :]
            before = (before_ref[pl.ds(mine, HALF), :], before_ref[C:, :])
            after = (after_ref[pl.ds(mine, HALF), :], after_ref[C:, :])
        else:
            cells = swap_ref[:HALF, :]
            before = (halo_ref[0, pl.ds(mine, HALF), :], halo_ref[0, C:, :])
            after = (halo_ref[1, pl.ds(mine, HALF), :], halo_ref[1, C:, :])
        fill(ext, HALF, cells, before, after, groups)
        for a in range(3):
            for b in range(3):
                win[3 * a + b, :, S * seg:S * (seg + 1)] = window(ext, (0, HALF), a - 1, b - 1, masks)
    peak = jnp.zeros((8, 128), f32)
    for t in range(TAPS):
        part = lax.dot_general(cot[...], win[t], (((1,), (1,)), ((), ())), preferred_element_type=f32)
        for o in range(64):
            xl, z, y = o // 32, (o // 4) % 8, o % 4
            for xh in range(2):
                block = part[8 * o:8 * o + 8, 128 * xh:128 * xh + 128]
                out_ref[y, xh, xl, z, 8 * t:8 * t + 8, :] = block
                peak = jnp.maximum(peak, jnp.abs(block))
    peak_ref[0] = peak
    bias_peak = jnp.zeros((8, 128), f32)
    total = jnp.zeros((C, 128), f32)
    for k in range(2 * S // 128):
        total = total + cot[:, 128 * k:128 * (k + 1)].astype(f32)
    total = jnp.broadcast_to(jnp.sum(total, axis=1, keepdims=True), (C, 128))
    for o in range(64):
        xl, z, y = o // 32, (o // 4) % 8, o % 4
        block = total[8 * o:8 * o + 8, :]
        bias_peak = jnp.maximum(bias_peak, jnp.abs(block))
        for xh in range(2):
            out_ref[y, xh, xl, z, 72:80, :] = block
    peak_ref[1] = bias_peak


def kernel_gradient(core, f, g, before, after, swapped, halo):
    return pl.pallas_call(
        dw_kernel,
        out_shape=(
            jax.ShapeDtypeStruct((4, 2, 2, 8, ROWS, 128), f32),
            jax.ShapeDtypeStruct((2, 8, 128), f32),
        ),
        in_specs=[smem()] + [vmem()] * 6,
        out_specs=(vmem(), vmem()),
        scratch_shapes=[
            pltpu.VMEM((HALF, 1152), bf16),
            pltpu.VMEM((TAPS, HALF, 2 * S), bf16),
            pltpu.VMEM((C, 2 * S), bf16),
        ],
        compiler_params=params(),
        cost_estimate=pl.CostEstimate(flops=2 * TAPS * C * HALF * 2 * S, bytes_accessed=9_000_000, transcendentals=0),
        name="kernel_gradient",
    )(core, f, g, before, after, swapped, halo)


def conv_kernel(core_ref, f_ref, g_ref, fb_ref, fa_ref, gb_ref, ga_ref, own_ref, other_ref, bias_ref,
                out_ref, grad_ref, ext, win, kern):
    core = core_ref[0]
    for half, ref in ((core, own_ref), (1 - core, other_ref)):
        for t in range(TAPS):
            lanes = pl.ds(pl.multiple_of(t * C + half * HALF, HALF), HALF)
            for xl in range(2):
                for z in range(8):
                    o = 256 * xl + 32 * z
                    kern[o:o + 32, lanes] = ref[z, xl, t]
    masks = column_masks(C)
    groups = (0, 1, 2, 3)
    fill(ext, C, f_ref[...], (fb_ref[:C, :], fb_ref[C:, :]), (fa_ref[:C, :], fa_ref[C:, :]), groups)
    for a in range(3):
        for b in range(3):
            t = 3 * a + b
            win[C * t:C * (t + 1), :] = window(ext, (0, C), a - 1, b - 1, masks)
    for m in range(2):
        rows = slice(HALF * m, HALF * (m + 1))
        total = jnp.dot(kern[rows, :], win[...], preferred_element_type=f32)
        out_ref[rows, :] = (total + bias_ref[rows, :]).astype(bf16)
    fill(ext, C, g_ref[...], (gb_ref[:C, :], gb_ref[C:, :]), (ga_ref[:C, :], ga_ref[C:, :]), groups)
    for a in range(3):
        for b in range(3):
            t = 3 * a + b
            win[C * t:C * (t + 1), :] = window(ext, (0, C), 1 - a, 1 - b, masks)
    for m in range(2):
        rows = slice(HALF * m, HALF * (m + 1))
        total = jnp.zeros((HALF, S), f32)
        for t in range(TAPS):
            total = total + lax.dot_general(
                kern[:, C * t + HALF * m:C * t + HALF * (m + 1)],
                win[C * t:C * (t + 1), :],
                (((0,), (0,)), ((), ())),
                preferred_element_type=f32,
            )
        grad_ref[rows, :] = total.astype(bf16)


def convolve(core, f, g, fb, fa, gb, ga, own, other, bias):
    flat = jax.ShapeDtypeStruct((C, S), bf16)
    return pl.pallas_call(
        conv_kernel,
        out_shape=(flat, flat),
        in_specs=[smem()] + [vmem()] * 9,
        out_specs=(vmem(), vmem()),
        scratch_shapes=[
            pltpu.VMEM((C, 1152), bf16),
            pltpu.VMEM((TAPS * C, S), bf16),
            pltpu.VMEM((C, TAPS * C), bf16),
        ],
        compiler_params=params(),
        cost_estimate=pl.CostEstimate(flops=4 * TAPS * C * C * S, bytes_accessed=9_000_000, transcendentals=0),
        name="convolve",
    )(core, f, g, fb, fa, gb, ga, own, other, bias)


def swap_cores(x):
    return lax.ppermute(x, "core", [(0, 1), (1, 0)])


def local(frames, weight, bias, cotangent):
    f = frames.reshape(C, S)
    g = cotangent.reshape(C, S)
    core = lax.axis_index("core")
    core_ref = core.reshape(1).astype(jnp.int32)
    up = [(i, i + 1) for i in range(63)]
    down = [(i + 1, i) for i in range(63)]

    fl, ff, gl, gf, swap = pack(core_ref, f, g)
    swapped = swap_cores(swap)
    fb = lax.ppermute(fl, CELLS, up)
    fa = lax.ppermute(ff, CELLS, down)
    halo = swap_cores(jnp.stack((fb, fa)))
    gb = lax.ppermute(gl, CELLS, up)
    ga = lax.ppermute(gf, CELLS, down)

    taps = weight.transpose(1, 2, 0, 3).reshape(TAPS, 32, C)
    half = lax.dynamic_slice_in_dim(taps, core * HALF, HALF, axis=2)
    beside = lax.ppermute(half, "xl", [(0, 1), (1, 0)])
    low = lax.axis_index("xl") == 0
    pair = jnp.stack((jnp.where(low, half, beside), jnp.where(low, beside, half)))
    own = lax.all_gather(pair, "z", axis=0, tiled=False)
    other = swap_cores(own)

    part, peak = kernel_gradient(core_ref, f, g, fb, fa, swapped, halo)
    peaks = jnp.maximum(jnp.max(peak, axis=(1, 2)), 1e-30)
    power = 14.0 - jnp.floor(jnp.log2(peaks))
    row = lax.broadcasted_iota(jnp.int32, (ROWS, 128), 0)
    lane = lax.broadcasted_iota(jnp.int32, (ROWS, 128), 1)
    factor = jnp.where(row < 72, jnp.exp2(power[0]), jnp.exp2(power[1]))
    scaled = part * factor
    scaled = jnp.where((row >= 72) & (lane == 126), power[0], scaled)
    scaled = jnp.where((row >= 72) & (lane == 127), power[1], scaled)
    sent = scaled.astype(f16).reshape(16, 8 * ROWS, 128)
    got = lax.all_to_all(sent, ("y", "xh", "xl"), 0, 0, tiled=True)
    got = got.reshape(16, 8, ROWS, 128).astype(f32)
    back_w = jnp.exp2(-got[:, 0, 72, 126])
    back_b = jnp.exp2(-got[:, 0, 72, 127])
    factors = jnp.where(row < 72, back_w[:, None, None], back_b[:, None, None])
    plane = jnp.sum(got * factors[:, None], axis=0)
    lines = lax.all_to_all(plane, "z", 0, 0, tiled=True)
    scale = 1.0 / math.sqrt(4 * 256 * 160)
    done = jnp.sum(lines, axis=0) * scale
    whole = lax.all_gather(done, ("y", "xh", "core"), axis=0, tiled=False)
    whole = whole.reshape(4, 2, 2, ROWS, 128)
    grad_weight = whole[:, :, :, :72].reshape(4, 2, 2, 3, 3, 8, 128)
    grad_weight = grad_weight.transpose(0, 5, 3, 4, 2, 1, 6).reshape(32, 3, 3, C)
    grad_bias = whole[:, 0, 0, 72:80, 0].reshape(32)

    outputs, grad_frames = convolve(core_ref, f, g, fb, fa, gb, ga, own, other, bias.reshape(C, 1))
    return (outputs.reshape(C, 1, S), grad_frames.reshape(C, 1, S), grad_weight, grad_bias)


def solution(mesh):
    fine = Mesh(mesh.devices.reshape(SIZES), AXES)
    cells = P(None, "y", CELLS)
    rows = ("xl", "z")
    in_specs = (cells, P(rows, None, None, None), P(), cells)
    out_specs = (cells, cells, P(rows, None, None, None), P(rows))
    return jax.shard_map(local, mesh=fine, in_specs=in_specs, out_specs=out_specs, check_vma=False)
```

```python
import functools
import math

import jax
import jax.numpy as jnp
from jax import lax
from jax.experimental import pallas as pl
from jax.experimental.pallas import tpu as pltpu
from jax.sharding import Mesh, PartitionSpec as P

C = 512
HALF = 256
W = 160
S = 640
TAPS = 9
AXES = ("y", "xh", "core", "xl", "z")
SIZES = (4, 2, 2, 2, 8)
CELLS = ("xh", "core", "xl", "z")

bf16 = jnp.bfloat16
f16 = jnp.float16
f32 = jnp.float32


def vmem():
    return pl.BlockSpec(memory_space=pltpu.VMEM)


def smem():
    return pl.BlockSpec(memory_space=pltpu.SMEM)


def params(mib):
    return pltpu.CompilerParams(vmem_limit_bytes=mib * 1024 * 1024)


def roll(x, shift):
    return pltpu.roll(x, shift % x.shape[-1], x.ndim - 1)


def pack_row(wide, tile, start):
    lane = lax.broadcasted_iota(jnp.int32, (128, 128), 1)
    tile = tile.astype(f32)
    total = jnp.zeros((128, 128), f32)
    for g in range(4):
        part = roll(tile[128 * g:128 * (g + 1)], 32 * g - start)
        total = jnp.where((lane >= 32 * g) & (lane < 32 * g + 32), part, total)
    return jnp.concatenate([wide, total.astype(bf16)], axis=0)


def pack_kernel(core_ref, f_ref, g_ref, fl_ref, ff_ref, gl_ref, gf_ref, swap_ref):
    for x, last, first in ((f_ref, fl_ref, ff_ref), (g_ref, gl_ref, gf_ref)):
        last[...] = pack_row(x[:, 512:640], x[:, 384:512], 96)
        first[...] = pack_row(x[:, 0:128], x[:, 128:256], 0)
    other = pl.multiple_of((1 - core_ref[0]) * HALF, HALF)
    swap_ref[:HALF, :] = f_ref[pl.ds(other, HALF), :]
    swap_ref[HALF:, :] = g_ref[...]


def pack(core, f, g):
    row = jax.ShapeDtypeStruct((640, 128), bf16)
    return pl.pallas_call(
        pack_kernel,
        out_shape=(row, row, row, row, jax.ShapeDtypeStruct((HALF + C, S), bf16)),
        in_specs=[smem(), vmem(), vmem()],
        out_specs=(vmem(),) * 5,
        compiler_params=params(12),
        name="pack",
    )(core, f, g)


def column_masks(rows):
    column = lax.broadcasted_iota(jnp.int32, (rows, S), 1) % W
    return column != 0, None, column != W - 1


def fill(ext, rows, cells, before, after, groups):
    ext[:rows, 256:896] = cells
    ext[:rows, 128:256] = before[0]
    ext[:rows, 896:1024] = after[0]
    tail_before = before[1].astype(f32)
    tail_after = after[1].astype(f32)
    for k, g in enumerate(groups):
        ext[128 * k:128 * (k + 1), 0:128] = pltpu.roll(tail_before, (96 - 32 * g) % 128, 1).astype(bf16)
        ext[128 * k:128 * (k + 1), 1024:1152] = pltpu.roll(tail_after, (128 - 32 * g) % 128, 1).astype(bf16)


def window(ext, rows, da, db, masks):
    start = 256 + da * W + db
    x = ext[pl.ds(rows[0], rows[1]), :][:, start:start + S]
    mask = masks[db + 1]
    if mask is not None:
        x = jnp.where(mask, x, jnp.zeros_like(x))
    return x


def pair_rows(part, y, xh, xl, k):
    lanes = slice(128 * xh, 128 * xh + 128)
    o = 256 * xl + 64 * k + 8 * y
    return jnp.concatenate([part[o:o + 8, lanes], part[o + 32:o + 40, lanes]], axis=0)


def store_tap(out_ref, part, position, peak):
    for y in range(4):
        for xh in range(2):
            for xl in range(2):
                for k in range(4):
                    block = pair_rows(part, y, xh, xl, k)
                    row = 64 * position + 16 * k
                    out_ref[4 * y + 2 * xh + xl, row:row + 16, :] = block
                    peak = jnp.maximum(peak, jnp.abs(block))
    return peak


def power_of(peak):
    top = jnp.max(jnp.max(peak, axis=1, keepdims=True), axis=0, keepdims=True)
    return 14.0 - jnp.floor(jnp.log2(jnp.maximum(top, 1e-30)))


def contract(cot, win):
    return lax.dot_general(cot, win, (((1,), (1,)), ((), ())), preferred_element_type=f32)


def middle_kernel(core_ref, f_ref, g_ref, swap_ref, out_ref, ext, win, cot):
    core = core_ref[0]
    mine = pl.multiple_of(core * HALF, HALF)
    masks = column_masks(HALF)
    cot[:, :S] = g_ref[...]
    cot[:, S:] = swap_ref[HALF:, :]
    ext[...] = jnp.zeros_like(ext)
    for seg in range(2):
        ext[:, 256:896] = f_ref[pl.ds(mine, HALF), :] if seg == 0 else swap_ref[:HALF, :]
        for b in range(3):
            win[b, :, S * seg:S * (seg + 1)] = window(ext, (0, HALF), 0, b - 1, masks)
    peak = jnp.zeros((16, 128), f32)
    for b in range(3):
        peak = store_tap(out_ref, contract(cot[...], win[b]), b, peak)
    power = power_of(peak)
    factor = jnp.exp2(power)
    total = jnp.zeros((C, 128), f32)
    for k in range(2 * S // 128):
        total = total + cot[:, 128 * k:128 * (k + 1)].astype(f32)
    total = jnp.sum(total, axis=1, keepdims=True)
    bias_power = power_of(jnp.abs(total))
    total = jnp.broadcast_to(total * jnp.exp2(bias_power), (C, 128))
    lane = lax.broadcasted_iota(jnp.int32, (8, 128), 1)
    for y in range(4):
        for xl in range(2):
            extra = jnp.where(lane == 8, jnp.broadcast_to(power, (8, 128)), jnp.broadcast_to(bias_power, (8, 128)))
            for z in range(8):
                o = 256 * xl + 32 * z + 8 * y
                extra = jnp.where(lane == z, total[o:o + 8, :], extra)
            for xh in range(2):
                d = 4 * y + 2 * xh + xl
                out_ref[d, 192:208, :] = jnp.concatenate([extra, extra], axis=0)
    for d in range(16):
        out_ref[d, :192, :] = out_ref[d, :192, :] * factor


def middle_taps(core, f, g, swapped):
    return pl.pallas_call(
        middle_kernel,
        out_shape=jax.ShapeDtypeStruct((16, 208, 128), f32),
        in_specs=[smem()] + [vmem()] * 3,
        out_specs=vmem(),
        scratch_shapes=[
            pltpu.VMEM((HALF, 1152), bf16),
            pltpu.VMEM((3, HALF, 2 * S), bf16),
            pltpu.VMEM((C, 2 * S), bf16),
        ],
        compiler_params=params(20),
        cost_estimate=pl.CostEstimate(flops=2 * 3 * C * HALF * 2 * S, bytes_accessed=5_000_000, transcendentals=0),
        name="middle_taps",
    )(core, f, g, swapped)


def outer_kernel(core_ref, f_ref, g_ref, before_ref, after_ref, swap_ref, halo_ref, out_ref, ext, win, cot):
    core = core_ref[0]
    mine = pl.multiple_of(core * HALF, HALF)
    masks = column_masks(HALF)
    groups = (2 * core, 2 * core + 1)
    cot[:, :S] = g_ref[...]
    cot[:, S:] = swap_ref[HALF:, :]
    for seg in range(2):
        if seg == 0:
            cells = f_ref[pl.ds(mine, HALF), :]
            before = (before_ref[pl.ds(mine, HALF), :], before_ref[C:, :])
            after = (after_ref[pl.ds(mine, HALF), :], after_ref[C:, :])
        else:
            cells = swap_ref[:HALF, :]
            before = (halo_ref[0, pl.ds(mine, HALF), :], halo_ref[0, C:, :])
            after = (halo_ref[1, pl.ds(mine, HALF), :], halo_ref[1, C:, :])
        fill(ext, HALF, cells, before, after, groups)
        for a in range(2):
            for b in range(3):
                win[3 * a + b, :, S * seg:S * (seg + 1)] = window(ext, (0, HALF), 2 * a - 1, b - 1, masks)
    peak = jnp.zeros((16, 128), f32)
    for t in range(6):
        peak = store_tap(out_ref, contract(cot[...], win[t]), t, peak)
    power = power_of(peak)
    factor = jnp.exp2(power)
    for d in range(16):
        out_ref[d, :384, :] = out_ref[d, :384, :] * factor
        out_ref[d, 384:400, :] = jnp.broadcast_to(power, (16, 128))


def outer_taps(core, f, g, before, after, swapped, halo):
    return pl.pallas_call(
        outer_kernel,
        out_shape=jax.ShapeDtypeStruct((16, 400, 128), f32),
        in_specs=[smem()] + [vmem()] * 6,
        out_specs=vmem(),
        scratch_shapes=[
            pltpu.VMEM((HALF, 1152), bf16),
            pltpu.VMEM((6, HALF, 2 * S), bf16),
            pltpu.VMEM((C, 2 * S), bf16),
        ],
        compiler_params=params(24),
        cost_estimate=pl.CostEstimate(flops=2 * 6 * C * HALF * 2 * S, bytes_accessed=7_000_000, transcendentals=0),
        name="outer_taps",
    )(core, f, g, before, after, swapped, halo)


def load_kernel(place_ref, own_ref, other_ref, kern):
    core, low = place_ref[0], place_ref[1]
    for half, ref in ((core, own_ref), (1 - core, other_ref)):
        for t in range(TAPS):
            lanes = pl.ds(pl.multiple_of(t * C + half * HALF, HALF), HALF)
            for k in range(2):
                first = pl.multiple_of(HALF * (low if k == 0 else 1 - low), HALF)
                kern[pl.ds(first, HALF), lanes] = ref[:, k, t].reshape(HALF, HALF)


def forward_kernel(core_ref, f_ref, fb_ref, fa_ref, own_ref, other_ref, bias_ref, out_ref, ext, win, kern):
    load_kernel(core_ref, own_ref, other_ref, kern)
    masks = column_masks(C)
    fill(ext, C, f_ref[...], (fb_ref[:C, :], fb_ref[C:, :]), (fa_ref[:C, :], fa_ref[C:, :]), (0, 1, 2, 3))
    for a in range(3):
        for b in range(3):
            t = 3 * a + b
            win[C * t:C * (t + 1), :] = window(ext, (0, C), a - 1, b - 1, masks)
    for m in range(2):
        rows = slice(HALF * m, HALF * (m + 1))
        total = jnp.dot(kern[rows, :], win[...], preferred_element_type=f32)
        out_ref[rows, :] = (total + bias_ref[rows, :]).astype(bf16)


def backward_kernel(core_ref, g_ref, gb_ref, ga_ref, own_ref, other_ref, grad_ref, ext, win, kern):
    load_kernel(core_ref, own_ref, other_ref, kern)
    masks = column_masks(C)
    fill(ext, C, g_ref[...], (gb_ref[:C, :], gb_ref[C:, :]), (ga_ref[:C, :], ga_ref[C:, :]), (0, 1, 2, 3))
    for a in range(3):
        for b in range(3):
            t = 3 * a + b
            win[C * t:C * (t + 1), :] = window(ext, (0, C), 1 - a, 1 - b, masks)
    for m in range(2):
        total = jnp.zeros((HALF, S), f32)
        for t in range(TAPS):
            total = total + lax.dot_general(
                kern[:, C * t + HALF * m:C * t + HALF * (m + 1)],
                win[C * t:C * (t + 1), :],
                (((0,), (0,)), ((), ())),
                preferred_element_type=f32,
            )
        grad_ref[HALF * m:HALF * (m + 1), :] = total.astype(bf16)


def convolve(body, name, *args):
    return pl.pallas_call(
        body,
        out_shape=jax.ShapeDtypeStruct((C, S), bf16),
        in_specs=[smem()] + [vmem()] * (len(args) - 1),
        out_specs=vmem(),
        scratch_shapes=[
            pltpu.VMEM((C, 1152), bf16),
            pltpu.VMEM((TAPS * C, S), bf16),
            pltpu.VMEM((C, TAPS * C), bf16),
        ],
        compiler_params=params(32),
        cost_estimate=pl.CostEstimate(flops=2 * TAPS * C * C * S, bytes_accessed=7_000_000, transcendentals=0),
        name=name,
    )(*args)


def swap_cores(x):
    return lax.ppermute(x, "core", [(0, 1), (1, 0)])


def sum_sources(got, rows, power):
    factor = jnp.exp2(-power)[:, None, None]
    return jnp.sum(got[:, :rows].astype(f32) * factor, axis=0)


def after(values, *first):
    return lax.optimization_barrier((tuple(values), first))[0]


def local(frames, weight, bias, cotangent):
    f = frames.reshape(C, S)
    g = cotangent.reshape(C, S)
    core = lax.axis_index("core")
    place = jnp.stack((core, lax.axis_index("xl"))).astype(jnp.int32)
    up = [(i, i + 1) for i in range(63)]
    down = [(i + 1, i) for i in range(63)]
    plane = ("y", "xh", "xl")

    fl, ff, gl, gf, swap = pack(place, f, g)
    swapped = swap_cores(swap)
    taps = weight.transpose(1, 2, 0, 3).reshape(TAPS, 32, C)
    half = lax.dynamic_slice_in_dim(taps, core * HALF, HALF, axis=2)
    (half,) = after((half,), fl)
    beside = lax.ppermute(half, "xl", [(0, 1), (1, 0)])
    fl, ff = after((fl, ff), swapped)
    fb = lax.ppermute(fl, CELLS, up)
    fa = lax.ppermute(ff, CELLS, down)

    part = middle_taps(place, f, g, swapped)
    part, fb, fa = lax.optimization_barrier((part, fb, fa))
    got = lax.all_to_all(part.astype(f16), plane, 0, 0, tiled=True)
    halo = swap_cores(jnp.stack((fb, fa)))

    half, beside = after((half, beside), fb, fa)
    own = lax.all_gather(jnp.stack((half, beside)), "z", axis=0, tiled=False)
    other = swap_cores(own)

    part2 = outer_taps(place, f, g, fb, fa, swapped, halo)
    got2 = lax.all_to_all(part2.astype(f16), plane, 0, 0, tiled=True)
    gl, gf = after((gl, gf), part2)
    gb = lax.ppermute(gl, CELLS, up)
    ga = lax.ppermute(gf, CELLS, down)

    extra, extra2 = lax.optimization_barrier((got[:, 192:200], got2[:, 384:392]))
    extra = extra.astype(f32)
    extra2 = extra2.astype(f32)
    middle = sum_sources(got, 192, extra[:, 0, 8]).reshape(3, 8, 8, 128)
    outer = sum_sources(got2, 384, extra2[:, 0, 8]).reshape(6, 8, 8, 128)
    ends = jnp.sum(extra * jnp.exp2(-extra[:, 0, 9])[:, None, None], axis=0)
    ends = jnp.broadcast_to(ends[:, :8].T[:, :, None], (8, 8, 128))[None]
    line = jnp.concatenate((outer[:3], middle, outer[3:], ends), axis=0).transpose(1, 0, 2, 3)
    lines = lax.all_to_all(line, "z", 0, 0, tiled=True)
    (f,) = after((f,), line, gb, ga)
    outputs = convolve(forward_kernel, "forward", place, f, fb, fa, own, other, bias.reshape(C, 1))
    lines, outputs = lax.optimization_barrier((lines, outputs))
    scale = 1.0 / math.sqrt(4 * 256 * 160)
    done = jnp.sum(lines, axis=0) * scale
    whole = jnp.broadcast_to(done, (16, 10, 8, 128))
    whole, g = lax.optimization_barrier((whole, g))
    whole = lax.all_to_all(whole, ("y", "xh", "core"), 0, 0, tiled=True)
    grad_frames = convolve(backward_kernel, "backward", place, g, gb, ga, own, other)
    whole, grad_frames = lax.optimization_barrier((whole, grad_frames))
    whole = whole.reshape(4, 2, 2, 10, 8, 128)
    grad_weight = whole[:, :, :, :9].reshape(4, 2, 2, 3, 3, 8, 128)
    grad_weight = grad_weight.transpose(0, 5, 3, 4, 2, 1, 6).reshape(32, 3, 3, C)
    grad_bias = whole[:, 0, 0, 9, :, 0].reshape(32)
    return (outputs.reshape(C, 1, S), grad_frames.reshape(C, 1, S), grad_weight, grad_bias)


def solution(mesh):
    fine = Mesh(mesh.devices.reshape(SIZES), AXES)
    cells = P(None, "y", CELLS)
    rows = ("xl", "z")
    in_specs = (cells, P(rows, None, None, None), P(), cells)
    out_specs = (cells, cells, P(rows, None, None, None), P(rows))
    return jax.shard_map(local, mesh=fine, in_specs=in_specs, out_specs=out_specs, check_vma=False)
```

```python
import functools
import math

import jax
import jax.numpy as jnp
from jax import lax
from jax.experimental import pallas as pl
from jax.experimental.pallas import tpu as pltpu
from jax.sharding import Mesh, PartitionSpec as P

C = 512
HALF = 256
W = 160
S = 640
TAPS = 9
GROUPS = (0, 1, 2, 3)
AXES = ("y", "xh", "core", "xl", "z")
SIZES = (4, 2, 2, 2, 8)
CELLS = ("xh", "core", "xl", "z")

bf16 = jnp.bfloat16
f16 = jnp.float16
f32 = jnp.float32


def vmem():
    return pl.BlockSpec(memory_space=pltpu.VMEM)


def smem():
    return pl.BlockSpec(memory_space=pltpu.SMEM)


def params(mib):
    return pltpu.CompilerParams(vmem_limit_bytes=mib * 1024 * 1024)


def roll(x, shift):
    return pltpu.roll(x, shift % x.shape[-1], x.ndim - 1)


def pack_row(wide, tile, start):
    lane = lax.broadcasted_iota(jnp.int32, (128, 128), 1)
    tile = tile.astype(f32)
    total = jnp.zeros((128, 128), f32)
    for g in range(4):
        part = roll(tile[128 * g:128 * (g + 1)], 32 * g - start)
        total = jnp.where((lane >= 32 * g) & (lane < 32 * g + 32), part, total)
    return jnp.concatenate([wide, total.astype(bf16)], axis=0)


def pack_kernel(f_ref, g_ref, last_ref, first_ref):
    for k, x in enumerate((f_ref, g_ref)):
        last_ref[k] = pack_row(x[:, 512:640], x[:, 384:512], 96)
        first_ref[k] = pack_row(x[:, 0:128], x[:, 128:256], 0)


def pack(f, g):
    rows = jax.ShapeDtypeStruct((2, 640, 128), bf16)
    return pl.pallas_call(
        pack_kernel,
        out_shape=(rows, rows),
        in_specs=[vmem(), vmem()],
        out_specs=(vmem(), vmem()),
        compiler_params=params(12),
        name="pack",
    )(f, g)


def column_masks(rows):
    column = lax.broadcasted_iota(jnp.int32, (rows, S), 1) % W
    return column != 0, None, column != W - 1


def fill(ext, rows, cells, before, after, groups):
    ext[:rows, 256:896] = cells
    ext[:rows, 128:256] = before[0]
    ext[:rows, 896:1024] = after[0]
    tail_before = before[1].astype(f32)
    tail_after = after[1].astype(f32)
    for k, g in enumerate(groups):
        ext[128 * k:128 * (k + 1), 0:128] = pltpu.roll(tail_before, (96 - 32 * g) % 128, 1).astype(bf16)
        ext[128 * k:128 * (k + 1), 1024:1152] = pltpu.roll(tail_after, (128 - 32 * g) % 128, 1).astype(bf16)


def window(ext, rows, da, db, masks):
    start = 256 + da * W + db
    x = ext[pl.ds(rows[0], rows[1]), :][:, start:start + S]
    mask = masks[db + 1]
    if mask is not None:
        x = jnp.where(mask, x, jnp.zeros_like(x))
    return x


def pair_rows(part, y, xh, xl, k):
    lanes = slice(128 * xh, 128 * xh + 128)
    o = 256 * xl + 64 * k + 8 * y
    return jnp.concatenate([part[o:o + 8, lanes], part[o + 32:o + 40, lanes]], axis=0)


def store_tap(out_ref, part, position, peak):
    for y in range(4):
        for xh in range(2):
            for xl in range(2):
                for k in range(4):
                    block = pair_rows(part, y, xh, xl, k)
                    row = 64 * position + 16 * k
                    out_ref[4 * y + 2 * xh + xl, row:row + 16, :] = block
                    peak = jnp.maximum(peak, jnp.abs(block))
    return peak


def power_of(peak):
    top = jnp.max(jnp.max(peak, axis=1, keepdims=True), axis=0, keepdims=True)
    return 14.0 - jnp.floor(jnp.log2(jnp.maximum(top, 1e-30)))


def contract(cot, win):
    return lax.dot_general(cot, win, (((1,), (1,)), ((), ())), preferred_element_type=f32)


def middle_kernel(core_ref, f_ref, g_ref, fx_ref, gx_ref, out_ref, ext, win, cot):
    core = core_ref[0]
    mine = pl.multiple_of(core * HALF, HALF)
    masks = column_masks(HALF)
    cot[:, :S] = g_ref[...]
    cot[:, S:] = gx_ref[...]
    ext[...] = jnp.zeros_like(ext)
    for seg in range(2):
        ext[:, 256:896] = (f_ref, fx_ref)[seg][pl.ds(mine, HALF), :]
        for b in range(3):
            win[b, :, S * seg:S * (seg + 1)] = window(ext, (0, HALF), 0, b - 1, masks)
    peak = jnp.zeros((16, 128), f32)
    for b in range(3):
        peak = store_tap(out_ref, contract(cot[...], win[b]), b, peak)
    power = power_of(peak)
    factor = jnp.exp2(power)
    total = jnp.zeros((C, 128), f32)
    for k in range(2 * S // 128):
        total = total + cot[:, 128 * k:128 * (k + 1)].astype(f32)
    total = jnp.sum(total, axis=1, keepdims=True)
    bias_power = power_of(jnp.abs(total))
    total = jnp.broadcast_to(total * jnp.exp2(bias_power), (C, 128))
    lane = lax.broadcasted_iota(jnp.int32, (8, 128), 1)
    for y in range(4):
        for xl in range(2):
            extra = jnp.where(lane == 8, jnp.broadcast_to(power, (8, 128)), jnp.broadcast_to(bias_power, (8, 128)))
            for z in range(8):
                o = 256 * xl + 32 * z + 8 * y
                extra = jnp.where(lane == z, total[o:o + 8, :], extra)
            for xh in range(2):
                d = 4 * y + 2 * xh + xl
                out_ref[d, 192:208, :] = jnp.concatenate([extra, extra], axis=0)
    for d in range(16):
        out_ref[d, :192, :] = out_ref[d, :192, :] * factor


def middle_taps(core, f, g, fx, gx):
    return pl.pallas_call(
        middle_kernel,
        out_shape=jax.ShapeDtypeStruct((16, 208, 128), f32),
        in_specs=[smem()] + [vmem()] * 4,
        out_specs=vmem(),
        scratch_shapes=[
            pltpu.VMEM((HALF, 1152), bf16),
            pltpu.VMEM((3, HALF, 2 * S), bf16),
            pltpu.VMEM((C, 2 * S), bf16),
        ],
        compiler_params=params(20),
        cost_estimate=pl.CostEstimate(flops=2 * 3 * C * HALF * 2 * S, bytes_accessed=5_000_000, transcendentals=0),
        name="middle_taps",
    )(core, f, g, fx, gx)


def outer_kernel(core_ref, f_ref, g_ref, before_ref, after_ref, fx_ref, gx_ref, halo_ref, out_ref, ext, win, cot):
    core = core_ref[0]
    mine = pl.multiple_of(core * HALF, HALF)
    masks = column_masks(HALF)
    groups = (2 * core, 2 * core + 1)
    cot[:, :S] = g_ref[...]
    cot[:, S:] = gx_ref[...]
    for seg in range(2):
        if seg == 0:
            cells = f_ref[pl.ds(mine, HALF), :]
            before = (before_ref[0, pl.ds(mine, HALF), :], before_ref[0, C:, :])
            after = (after_ref[0, pl.ds(mine, HALF), :], after_ref[0, C:, :])
        else:
            cells = fx_ref[pl.ds(mine, HALF), :]
            before = (halo_ref[0, pl.ds(mine, HALF), :], halo_ref[0, C:, :])
            after = (halo_ref[1, pl.ds(mine, HALF), :], halo_ref[1, C:, :])
        fill(ext, HALF, cells, before, after, groups)
        for a in range(2):
            for b in range(3):
                win[3 * a + b, :, S * seg:S * (seg + 1)] = window(ext, (0, HALF), 2 * a - 1, b - 1, masks)
    peak = jnp.zeros((16, 128), f32)
    for t in range(6):
        peak = store_tap(out_ref, contract(cot[...], win[t]), t, peak)
    power = power_of(peak)
    factor = jnp.exp2(power)
    for d in range(16):
        out_ref[d, :384, :] = out_ref[d, :384, :] * factor
        out_ref[d, 384:400, :] = jnp.broadcast_to(power, (16, 128))


def outer_taps(core, f, g, before, after, fx, gx, halo):
    return pl.pallas_call(
        outer_kernel,
        out_shape=jax.ShapeDtypeStruct((16, 400, 128), f32),
        in_specs=[smem()] + [vmem()] * 7,
        out_specs=vmem(),
        scratch_shapes=[
            pltpu.VMEM((HALF, 1152), bf16),
            pltpu.VMEM((6, HALF, 2 * S), bf16),
            pltpu.VMEM((C, 2 * S), bf16),
        ],
        compiler_params=params(24),
        cost_estimate=pl.CostEstimate(flops=2 * 6 * C * HALF * 2 * S, bytes_accessed=7_000_000, transcendentals=0),
        name="outer_taps",
    )(core, f, g, before, after, fx, gx, halo)


def load_kernel(place_ref, own_ref, other_ref, kern):
    core, low = place_ref[0], place_ref[1]
    for half, ref in ((core, own_ref), (1 - core, other_ref)):
        for t in range(TAPS):
            lanes = pl.ds(pl.multiple_of(t * C + half * HALF, HALF), HALF)
            for k in range(2):
                first = pl.multiple_of(HALF * (low if k == 0 else 1 - low), HALF)
                kern[pl.ds(first, HALF), lanes] = ref[:, k, t].reshape(HALF, HALF)


def forward_kernel(core_ref, f_ref, before_ref, after_ref, own_ref, other_ref, bias_ref, out_ref, ext, win, kern):
    load_kernel(core_ref, own_ref, other_ref, kern)
    masks = column_masks(C)
    fill(ext, C, f_ref[...], (before_ref[0, :C, :], before_ref[0, C:, :]), (after_ref[0, :C, :], after_ref[0, C:, :]), GROUPS)
    for a in range(3):
        for b in range(3):
            t = 3 * a + b
            win[C * t:C * (t + 1), :] = window(ext, (0, C), a - 1, b - 1, masks)
    for m in range(2):
        rows = slice(HALF * m, HALF * (m + 1))
        total = jnp.dot(kern[rows, :], win[...], preferred_element_type=f32)
        out_ref[rows, :] = (total + bias_ref[rows, :]).astype(bf16)


def backward_kernel(core_ref, g_ref, before_ref, after_ref, own_ref, other_ref, grad_ref, ext, win, kern):
    load_kernel(core_ref, own_ref, other_ref, kern)
    masks = column_masks(C)
    fill(ext, C, g_ref[...], (before_ref[1, :C, :], before_ref[1, C:, :]), (after_ref[1, :C, :], after_ref[1, C:, :]), GROUPS)
    for a in range(3):
        for b in range(3):
            t = 3 * a + b
            win[C * t:C * (t + 1), :] = window(ext, (0, C), 1 - a, 1 - b, masks)
    for m in range(2):
        total = jnp.zeros((HALF, S), f32)
        for t in range(TAPS):
            total = total + lax.dot_general(
                kern[:, C * t + HALF * m:C * t + HALF * (m + 1)],
                win[C * t:C * (t + 1), :],
                (((0,), (0,)), ((), ())),
                preferred_element_type=f32,
            )
        grad_ref[HALF * m:HALF * (m + 1), :] = total.astype(bf16)


def convolve(body, name, *args):
    return pl.pallas_call(
        body,
        out_shape=jax.ShapeDtypeStruct((C, S), bf16),
        in_specs=[smem()] + [vmem()] * (len(args) - 1),
        out_specs=vmem(),
        scratch_shapes=[
            pltpu.VMEM((C, 1152), bf16),
            pltpu.VMEM((TAPS * C, S), bf16),
            pltpu.VMEM((C, TAPS * C), bf16),
        ],
        compiler_params=params(32),
        cost_estimate=pl.CostEstimate(flops=2 * TAPS * C * C * S, bytes_accessed=7_000_000, transcendentals=0),
        name=name,
    )(*args)


def swap_cores(x):
    return lax.ppermute(x, "core", [(0, 1), (1, 0)])


def sum_sources(got, rows, power):
    factor = jnp.exp2(-power)[:, None, None]
    return jnp.sum(got[:, :rows].astype(f32) * factor, axis=0)


def after(values, *first):
    return lax.optimization_barrier((tuple(values), first))[0]


def local(frames, weight, bias, cotangent):
    f = frames.reshape(C, S)
    g = cotangent.reshape(C, S)
    core = lax.axis_index("core")
    place = jnp.stack((core, lax.axis_index("xl"))).astype(jnp.int32)
    up = [(i, i + 1) for i in range(63)]
    down = [(i + 1, i) for i in range(63)]
    plane = ("y", "xh", "xl")

    fx = swap_cores(f)
    gx = swap_cores(g)
    last, first = pack(f, g)
    above = lax.ppermute(last, CELLS, up)
    below = lax.ppermute(first, CELLS, down)

    part = middle_taps(place, f, g, fx, gx)
    sent = part.astype(f16)
    got = lax.all_to_all(sent, plane, 0, 0, tiled=True)
    near = after((above[0], below[0]), sent)
    halo = swap_cores(jnp.stack(near))

    taps = weight.transpose(1, 2, 0, 3).reshape(TAPS, 32, C)
    half = lax.dynamic_slice_in_dim(taps, core * HALF, HALF, axis=2)
    beside = lax.ppermute(half, "xl", [(0, 1), (1, 0)])
    half, beside = after((half, beside), above, below, sent)
    own = lax.all_gather(jnp.stack((half, beside)), "z", axis=0, tiled=False)

    part2 = outer_taps(place, f, g, above, below, fx, gx, halo)
    got2 = lax.all_to_all(part2.astype(f16), plane, 0, 0, tiled=True)
    other = swap_cores(own)

    extra = lax.optimization_barrier(got[:, 192:200]).astype(f32)
    extra2 = lax.optimization_barrier(got2[:, 384:392]).astype(f32)
    middle = sum_sources(got, 192, extra[:, 0, 8]).reshape(3, 8, 8, 128)
    outer = sum_sources(got2, 384, extra2[:, 0, 8]).reshape(6, 8, 8, 128)
    ends = jnp.sum(extra * jnp.exp2(-extra[:, 0, 9])[:, None, None], axis=0)
    ends = jnp.broadcast_to(ends[:, :8].T[:, :, None], (8, 8, 128))[None]
    line = jnp.concatenate((outer[:3], middle, outer[3:], ends), axis=0).transpose(1, 0, 2, 3)
    lines = lax.all_to_all(line, "z", 0, 0, tiled=True)
    (f,) = after((f,), line)
    outputs = convolve(forward_kernel, "forward", place, f, above, below, own, other, bias.reshape(C, 1))
    lines, outputs = lax.optimization_barrier((lines, outputs))
    scale = 1.0 / math.sqrt(4 * 256 * 160)
    done = jnp.sum(lines, axis=0) * scale
    whole = jnp.broadcast_to(done, (16, 10, 8, 128))
    whole, g = lax.optimization_barrier((whole, g))
    whole = lax.all_to_all(whole, ("y", "xh", "core"), 0, 0, tiled=True)
    grad_frames = convolve(backward_kernel, "backward", place, g, above, below, own, other)
    whole, grad_frames = lax.optimization_barrier((whole, grad_frames))
    whole = whole.reshape(4, 2, 2, 10, 8, 128)
    grad_weight = whole[:, :, :, :9].reshape(4, 2, 2, 3, 3, 8, 128)
    grad_weight = grad_weight.transpose(0, 5, 3, 4, 2, 1, 6).reshape(32, 3, 3, C)
    grad_bias = whole[:, 0, 0, 9, :, 0].reshape(32)
    return (outputs.reshape(C, 1, S), grad_frames.reshape(C, 1, S), grad_weight, grad_bias)


def solution(mesh):
    fine = Mesh(mesh.devices.reshape(SIZES), AXES)
    cells = P(None, "y", CELLS)
    rows = ("xl", "z")
    in_specs = (cells, P(rows, None, None, None), P(), cells)
    out_specs = (cells, cells, P(rows, None, None, None), P(rows))
    return jax.shard_map(local, mesh=fine, in_specs=in_specs, out_specs=out_specs, check_vma=False)
```

```python
import functools
import math

import jax
import jax.numpy as jnp
from jax import lax
from jax.experimental import pallas as pl
from jax.experimental.pallas import tpu as pltpu
from jax.sharding import Mesh, PartitionSpec as P

C = 512
HALF = 256
W = 160
S = 640
TAPS = 9
GROUPS = (0, 1, 2, 3)
AXES = ("y", "xh", "core", "xl", "z")
SIZES = (4, 2, 2, 2, 8)
CELLS = ("xh", "core", "xl", "z")

bf16 = jnp.bfloat16
f16 = jnp.float16
f32 = jnp.float32


def vmem():
    return pl.BlockSpec(memory_space=pltpu.VMEM)


def smem():
    return pl.BlockSpec(memory_space=pltpu.SMEM)


def params(mib):
    return pltpu.CompilerParams(vmem_limit_bytes=mib * 1024 * 1024)


def roll(x, shift):
    return pltpu.roll(x, shift % x.shape[-1], x.ndim - 1)


def pack_row(wide, tile, start):
    lane = lax.broadcasted_iota(jnp.int32, (128, 128), 1)
    tile = tile.astype(f32)
    total = jnp.zeros((128, 128), f32)
    for g in range(4):
        part = roll(tile[128 * g:128 * (g + 1)], 32 * g - start)
        total = jnp.where((lane >= 32 * g) & (lane < 32 * g + 32), part, total)
    return jnp.concatenate([wide, total.astype(bf16)], axis=0)


def pack_kernel(f_ref, g_ref, last_ref, first_ref):
    for k, x in enumerate((f_ref, g_ref)):
        last_ref[k] = pack_row(x[:, 512:640], x[:, 384:512], 96)
        first_ref[k] = pack_row(x[:, 0:128], x[:, 128:256], 0)


def pack(f, g):
    rows = jax.ShapeDtypeStruct((2, 640, 128), bf16)
    return pl.pallas_call(
        pack_kernel,
        out_shape=(rows, rows),
        in_specs=[vmem(), vmem()],
        out_specs=(vmem(), vmem()),
        compiler_params=params(12),
        name="pack",
    )(f, g)


def column_masks(rows):
    column = lax.broadcasted_iota(jnp.int32, (rows, S), 1) % W
    return column != 0, None, column != W - 1


def fill(ext, rows, cells, before, after, groups):
    ext[:rows, 256:896] = cells
    ext[:rows, 128:256] = before[0]
    ext[:rows, 896:1024] = after[0]
    tail_before = before[1].astype(f32)
    tail_after = after[1].astype(f32)
    for k, g in enumerate(groups):
        ext[128 * k:128 * (k + 1), 0:128] = pltpu.roll(tail_before, (96 - 32 * g) % 128, 1).astype(bf16)
        ext[128 * k:128 * (k + 1), 1024:1152] = pltpu.roll(tail_after, (128 - 32 * g) % 128, 1).astype(bf16)


def window(ext, rows, da, db, masks):
    start = 256 + da * W + db
    x = ext[pl.ds(rows[0], rows[1]), :][:, start:start + S]
    mask = masks[db + 1]
    if mask is not None:
        x = jnp.where(mask, x, jnp.zeros_like(x))
    return x


def pair_rows(part, y, xh, xl, k):
    lanes = slice(128 * xh, 128 * xh + 128)
    o = 256 * xl + 64 * k + 8 * y
    return jnp.concatenate([part[o:o + 8, lanes], part[o + 32:o + 40, lanes]], axis=0)


def store_tap(out_ref, part, position, peak):
    for y in range(4):
        for xh in range(2):
            for xl in range(2):
                for k in range(4):
                    block = pair_rows(part, y, xh, xl, k)
                    row = 64 * position + 16 * k
                    out_ref[4 * y + 2 * xh + xl, row:row + 16, :] = block
                    peak = jnp.maximum(peak, jnp.abs(block))
    return peak


def power_of(peak):
    top = jnp.max(jnp.max(peak, axis=1, keepdims=True), axis=0, keepdims=True)
    return 14.0 - jnp.floor(jnp.log2(jnp.maximum(top, 1e-30)))


def contract(cot, win):
    return lax.dot_general(cot, win, (((1,), (1,)), ((), ())), preferred_element_type=f32)


def middle_kernel(core_ref, f_ref, g_ref, fx_ref, gx_ref, out_ref, ext, win, cot):
    core = core_ref[0]
    mine = pl.multiple_of(core * HALF, HALF)
    masks = column_masks(HALF)
    cot[:, :S] = g_ref[...]
    cot[:, S:] = gx_ref[...]
    ext[...] = jnp.zeros_like(ext)
    for seg in range(2):
        ext[:, 256:896] = (f_ref, fx_ref)[seg][pl.ds(mine, HALF), :]
        for b in range(3):
            win[b, :, S * seg:S * (seg + 1)] = window(ext, (0, HALF), 0, b - 1, masks)
    peak = jnp.zeros((16, 128), f32)
    for b in range(3):
        peak = store_tap(out_ref, contract(cot[...], win[b]), b, peak)
    power = power_of(peak)
    factor = jnp.exp2(power)
    total = jnp.zeros((C, 128), f32)
    for k in range(2 * S // 128):
        total = total + cot[:, 128 * k:128 * (k + 1)].astype(f32)
    total = jnp.sum(total, axis=1, keepdims=True)
    bias_power = power_of(jnp.abs(total))
    total = jnp.broadcast_to(total * jnp.exp2(bias_power), (C, 128))
    lane = lax.broadcasted_iota(jnp.int32, (8, 128), 1)
    for y in range(4):
        for xl in range(2):
            extra = jnp.where(lane == 8, jnp.broadcast_to(power, (8, 128)), jnp.broadcast_to(bias_power, (8, 128)))
            for z in range(8):
                o = 256 * xl + 32 * z + 8 * y
                extra = jnp.where(lane == z, total[o:o + 8, :], extra)
            for xh in range(2):
                d = 4 * y + 2 * xh + xl
                out_ref[d, 192:208, :] = jnp.concatenate([extra, extra], axis=0)
    for d in range(16):
        out_ref[d, :192, :] = out_ref[d, :192, :] * factor


def middle_taps(core, f, g, fx, gx):
    return pl.pallas_call(
        middle_kernel,
        out_shape=jax.ShapeDtypeStruct((16, 208, 128), f32),
        in_specs=[smem()] + [vmem()] * 4,
        out_specs=vmem(),
        scratch_shapes=[
            pltpu.VMEM((HALF, 1152), bf16),
            pltpu.VMEM((3, HALF, 2 * S), bf16),
            pltpu.VMEM((C, 2 * S), bf16),
        ],
        compiler_params=params(20),
        cost_estimate=pl.CostEstimate(flops=2 * 3 * C * HALF * 2 * S, bytes_accessed=5_000_000, transcendentals=0),
        name="middle_taps",
    )(core, f, g, fx, gx)


def outer_kernel(core_ref, f_ref, g_ref, before_ref, after_ref, fx_ref, gx_ref, halo_ref, out_ref, ext, win, cot):
    core = core_ref[0]
    mine = pl.multiple_of(core * HALF, HALF)
    masks = column_masks(HALF)
    groups = (2 * core, 2 * core + 1)
    cot[:, :S] = g_ref[...]
    cot[:, S:] = gx_ref[...]
    for seg in range(2):
        if seg == 0:
            cells = f_ref[pl.ds(mine, HALF), :]
            before = (before_ref[0, pl.ds(mine, HALF), :], before_ref[0, C:, :])
            after = (after_ref[0, pl.ds(mine, HALF), :], after_ref[0, C:, :])
        else:
            cells = fx_ref[pl.ds(mine, HALF), :]
            before = (halo_ref[0, pl.ds(mine, HALF), :], halo_ref[0, C:, :])
            after = (halo_ref[1, pl.ds(mine, HALF), :], halo_ref[1, C:, :])
        fill(ext, HALF, cells, before, after, groups)
        for a in range(2):
            for b in range(3):
                win[3 * a + b, :, S * seg:S * (seg + 1)] = window(ext, (0, HALF), 2 * a - 1, b - 1, masks)
    peak = jnp.zeros((16, 128), f32)
    for t in range(6):
        peak = store_tap(out_ref, contract(cot[...], win[t]), t, peak)
    power = power_of(peak)
    factor = jnp.exp2(power)
    for d in range(16):
        out_ref[d, :384, :] = out_ref[d, :384, :] * factor
        out_ref[d, 384:400, :] = jnp.broadcast_to(power, (16, 128))


def outer_taps(core, f, g, before, after, fx, gx, halo):
    return pl.pallas_call(
        outer_kernel,
        out_shape=jax.ShapeDtypeStruct((16, 400, 128), f32),
        in_specs=[smem()] + [vmem()] * 7,
        out_specs=vmem(),
        scratch_shapes=[
            pltpu.VMEM((HALF, 1152), bf16),
            pltpu.VMEM((6, HALF, 2 * S), bf16),
            pltpu.VMEM((C, 2 * S), bf16),
        ],
        compiler_params=params(24),
        cost_estimate=pl.CostEstimate(flops=2 * 6 * C * HALF * 2 * S, bytes_accessed=7_000_000, transcendentals=0),
        name="outer_taps",
    )(core, f, g, before, after, fx, gx, halo)


def load_kernel(place_ref, own_ref, other_ref, kern):
    core, low = place_ref[0], place_ref[1]
    for half, ref in ((core, own_ref), (1 - core, other_ref)):
        for t in range(TAPS):
            lanes = pl.ds(pl.multiple_of(t * C + half * HALF, HALF), HALF)
            for k in range(2):
                first = pl.multiple_of(HALF * (low if k == 0 else 1 - low), HALF)
                kern[pl.ds(first, HALF), lanes] = ref[:, k, t].reshape(HALF, HALF)


def forward_kernel(core_ref, f_ref, before_ref, after_ref, own_ref, other_ref, bias_ref, out_ref, ext, win, kern):
    load_kernel(core_ref, own_ref, other_ref, kern)
    masks = column_masks(C)
    fill(ext, C, f_ref[...], (before_ref[0, :C, :], before_ref[0, C:, :]), (after_ref[0, :C, :], after_ref[0, C:, :]), GROUPS)
    for a in range(3):
        for b in range(3):
            t = 3 * a + b
            win[C * t:C * (t + 1), :] = window(ext, (0, C), a - 1, b - 1, masks)
    for m in range(2):
        rows = slice(HALF * m, HALF * (m + 1))
        total = jnp.dot(kern[rows, :], win[...], preferred_element_type=f32)
        out_ref[rows, :] = (total + bias_ref[rows, :]).astype(bf16)


def backward_kernel(core_ref, g_ref, before_ref, after_ref, own_ref, other_ref, grad_ref, ext, win, kern):
    load_kernel(core_ref, own_ref, other_ref, kern)
    masks = column_masks(C)
    fill(ext, C, g_ref[...], (before_ref[1, :C, :], before_ref[1, C:, :]), (after_ref[1, :C, :], after_ref[1, C:, :]), GROUPS)
    for a in range(3):
        for b in range(3):
            t = 3 * a + b
            win[C * t:C * (t + 1), :] = window(ext, (0, C), 1 - a, 1 - b, masks)
    for m in range(2):
        total = jnp.zeros((HALF, S), f32)
        for t in range(TAPS):
            total = total + lax.dot_general(
                kern[:, C * t + HALF * m:C * t + HALF * (m + 1)],
                win[C * t:C * (t + 1), :],
                (((0,), (0,)), ((), ())),
                preferred_element_type=f32,
            )
        grad_ref[HALF * m:HALF * (m + 1), :] = total.astype(bf16)


def convolve(body, name, *args):
    return pl.pallas_call(
        body,
        out_shape=jax.ShapeDtypeStruct((C, S), bf16),
        in_specs=[smem()] + [vmem()] * (len(args) - 1),
        out_specs=vmem(),
        scratch_shapes=[
            pltpu.VMEM((C, 1152), bf16),
            pltpu.VMEM((TAPS * C, S), bf16),
            pltpu.VMEM((C, TAPS * C), bf16),
        ],
        compiler_params=params(32),
        cost_estimate=pl.CostEstimate(flops=2 * TAPS * C * C * S, bytes_accessed=7_000_000, transcendentals=0),
        name=name,
    )(*args)


def swap_cores(x):
    return lax.ppermute(x, "core", [(0, 1), (1, 0)])


def sum_sources(got, rows, power):
    factor = jnp.exp2(-power)[:, None, None]
    return jnp.sum(got[:, :rows].astype(f32) * factor, axis=0)


def after(values, *first):
    return lax.optimization_barrier((tuple(values), first))[0]


def local(frames, weight, bias, cotangent):
    f = frames.reshape(C, S)
    g = cotangent.reshape(C, S)
    core = lax.axis_index("core")
    place = jnp.stack((core, lax.axis_index("xl"))).astype(jnp.int32)
    up = [(i, i + 1) for i in range(63)]
    down = [(i + 1, i) for i in range(63)]
    plane = ("y", "xh", "xl")

    taps = weight.transpose(1, 2, 0, 3).reshape(TAPS, 32, C)
    half = lax.dynamic_slice_in_dim(taps, core * HALF, HALF, axis=2)
    beside = lax.ppermute(half, "xl", [(0, 1), (1, 0)])

    fx = swap_cores(f)
    gx = swap_cores(g)
    last, first = pack(f, g)
    half, beside = after((half, beside), last, fx, gx)
    own = lax.all_gather(jnp.stack((half, beside)), "z", axis=0, tiled=False)
    above = lax.ppermute(last, CELLS, up)
    below = lax.ppermute(first, CELLS, down)

    part = middle_taps(place, f, g, fx, gx)
    sent = part.astype(f16)
    got = lax.all_to_all(sent, plane, 0, 0, tiled=True)
    above, below = after((above, below), sent)
    halo = swap_cores(jnp.stack((above[0], below[0])))

    part2 = outer_taps(place, f, g, above, below, fx, gx, halo)
    (sent2,) = after((part2.astype(f16),), got)
    got2 = lax.all_to_all(sent2, plane, 0, 0, tiled=True)
    (own,) = after((own,), got2)
    other = swap_cores(own)

    extra = lax.optimization_barrier(got[:, 192:200]).astype(f32)
    extra2 = lax.optimization_barrier(got2[:, 384:392]).astype(f32)
    middle = sum_sources(got, 192, extra[:, 0, 8]).reshape(3, 8, 8, 128)
    outer = sum_sources(got2, 384, extra2[:, 0, 8]).reshape(6, 8, 8, 128)
    ends = jnp.sum(extra * jnp.exp2(-extra[:, 0, 9])[:, None, None], axis=0)
    ends = jnp.broadcast_to(ends[:, :8].T[:, :, None], (8, 8, 128))[None]
    line = jnp.concatenate((outer[:3], middle, outer[3:], ends), axis=0).transpose(1, 0, 2, 3)
    lines = lax.all_to_all(line, "z", 0, 0, tiled=True)
    (f,) = after((f,), line)
    outputs = convolve(forward_kernel, "forward", place, f, above, below, own, other, bias.reshape(C, 1))
    lines, outputs = lax.optimization_barrier((lines, outputs))
    scale = 1.0 / math.sqrt(4 * 256 * 160)
    done = jnp.sum(lines, axis=0) * scale
    whole = jnp.broadcast_to(done, (16, 10, 8, 128))
    whole, g = lax.optimization_barrier((whole, g))
    whole = lax.all_to_all(whole, ("y", "xh", "core"), 0, 0, tiled=True)
    grad_frames = convolve(backward_kernel, "backward", place, g, above, below, own, other)
    whole, grad_frames = lax.optimization_barrier((whole, grad_frames))
    whole = whole.reshape(4, 2, 2, 10, 8, 128)
    grad_weight = whole[:, :, :, :9].reshape(4, 2, 2, 3, 3, 8, 128)
    grad_weight = grad_weight.transpose(0, 5, 3, 4, 2, 1, 6).reshape(32, 3, 3, C)
    grad_bias = whole[:, 0, 0, 9, :, 0].reshape(32)
    return (outputs.reshape(C, 1, S), grad_frames.reshape(C, 1, S), grad_weight, grad_bias)


def solution(mesh):
    fine = Mesh(mesh.devices.reshape(SIZES), AXES)
    cells = P(None, "y", CELLS)
    rows = ("xl", "z")
    in_specs = (cells, P(rows, None, None, None), P(), cells)
    out_specs = (cells, cells, P(rows, None, None, None), P(rows))
    return jax.shard_map(local, mesh=fine, in_specs=in_specs, out_specs=out_specs, check_vma=False)
```

```python
import functools
import math

import jax
import jax.numpy as jnp
from jax import lax
from jax.experimental import pallas as pl
from jax.experimental.pallas import tpu as pltpu
from jax.sharding import Mesh, PartitionSpec as P

C = 512
HALF = 256
W = 160
S = 640
TAPS = 9
GROUPS = (0, 1, 2, 3)
AXES = ("y", "xh", "core", "xl", "z")
SIZES = (4, 2, 2, 2, 8)
CELLS = ("xh", "core", "xl", "z")

bf16 = jnp.bfloat16
f16 = jnp.float16
f32 = jnp.float32


def vmem():
    return pl.BlockSpec(memory_space=pltpu.VMEM)


def smem():
    return pl.BlockSpec(memory_space=pltpu.SMEM)


def params(mib):
    return pltpu.CompilerParams(vmem_limit_bytes=mib * 1024 * 1024)


def roll(x, shift):
    return pltpu.roll(x, shift % x.shape[-1], x.ndim - 1)


def pack_row(wide, tile, start):
    lane = lax.broadcasted_iota(jnp.int32, (128, 128), 1)
    tile = tile.astype(f32)
    total = jnp.zeros((128, 128), f32)
    for g in range(4):
        part = roll(tile[128 * g:128 * (g + 1)], 32 * g - start)
        total = jnp.where((lane >= 32 * g) & (lane < 32 * g + 32), part, total)
    return jnp.concatenate([wide, total.astype(bf16)], axis=0)


def pack_kernel(f_ref, g_ref, last_ref, first_ref):
    for k, x in enumerate((f_ref, g_ref)):
        last_ref[k] = pack_row(x[:, 512:640], x[:, 384:512], 96)
        first_ref[k] = pack_row(x[:, 0:128], x[:, 128:256], 0)


def pack(f, g):
    rows = jax.ShapeDtypeStruct((2, 640, 128), bf16)
    return pl.pallas_call(
        pack_kernel,
        out_shape=(rows, rows),
        in_specs=[vmem(), vmem()],
        out_specs=(vmem(), vmem()),
        compiler_params=params(12),
        name="pack",
    )(f, g)


def column_masks(rows):
    column = lax.broadcasted_iota(jnp.int32, (rows, S), 1) % W
    return column != 0, None, column != W - 1


def fill(ext, rows, cells, before, after, groups):
    ext[:rows, 256:896] = cells
    ext[:rows, 128:256] = before[0]
    ext[:rows, 896:1024] = after[0]
    tail_before = before[1].astype(f32)
    tail_after = after[1].astype(f32)
    for k, g in enumerate(groups):
        ext[128 * k:128 * (k + 1), 0:128] = pltpu.roll(tail_before, (96 - 32 * g) % 128, 1).astype(bf16)
        ext[128 * k:128 * (k + 1), 1024:1152] = pltpu.roll(tail_after, (128 - 32 * g) % 128, 1).astype(bf16)


def window(ext, rows, da, db, masks):
    start = 256 + da * W + db
    x = ext[pl.ds(rows[0], rows[1]), :][:, start:start + S]
    mask = masks[db + 1]
    if mask is not None:
        x = jnp.where(mask, x, jnp.zeros_like(x))
    return x


def pair_rows(part, y, xh, xl, k):
    lanes = slice(128 * xh, 128 * xh + 128)
    o = 256 * xl + 64 * k + 8 * y
    return jnp.concatenate([part[o:o + 8, lanes], part[o + 32:o + 40, lanes]], axis=0)


def store_tap(out_ref, part, position, peak):
    for y in range(4):
        for xh in range(2):
            for xl in range(2):
                for k in range(4):
                    block = pair_rows(part, y, xh, xl, k)
                    row = 64 * position + 16 * k
                    out_ref[4 * y + 2 * xh + xl, row:row + 16, :] = block
                    peak = jnp.maximum(peak, jnp.abs(block))
    return peak


def power_of(peak):
    top = jnp.max(jnp.max(peak, axis=1, keepdims=True), axis=0, keepdims=True)
    return 14.0 - jnp.floor(jnp.log2(jnp.maximum(top, 1e-30)))


def contract(cot, win):
    return lax.dot_general(cot, win, (((1,), (1,)), ((), ())), preferred_element_type=f32)


def middle_kernel(core_ref, f_ref, g_ref, fx_ref, gx_ref, out_ref, ext, win, cot):
    core = core_ref[0]
    mine = pl.multiple_of(core * HALF, HALF)
    masks = column_masks(HALF)
    cot[:, :S] = g_ref[...]
    cot[:, S:] = gx_ref[...]
    ext[...] = jnp.zeros_like(ext)
    for seg in range(2):
        ext[:, 256:896] = (f_ref, fx_ref)[seg][pl.ds(mine, HALF), :]
        for b in range(3):
            win[b, :, S * seg:S * (seg + 1)] = window(ext, (0, HALF), 0, b - 1, masks)
    peak = jnp.zeros((16, 128), f32)
    for b in range(3):
        peak = store_tap(out_ref, contract(cot[...], win[b]), b, peak)
    power = power_of(peak)
    factor = jnp.exp2(power)
    total = jnp.zeros((C, 128), f32)
    for k in range(2 * S // 128):
        total = total + cot[:, 128 * k:128 * (k + 1)].astype(f32)
    total = jnp.sum(total, axis=1, keepdims=True)
    bias_power = power_of(jnp.abs(total))
    total = jnp.broadcast_to(total * jnp.exp2(bias_power), (C, 128))
    lane = lax.broadcasted_iota(jnp.int32, (8, 128), 1)
    for y in range(4):
        for xl in range(2):
            extra = jnp.where(lane == 8, jnp.broadcast_to(power, (8, 128)), jnp.broadcast_to(bias_power, (8, 128)))
            for z in range(8):
                o = 256 * xl + 32 * z + 8 * y
                extra = jnp.where(lane == z, total[o:o + 8, :], extra)
            for xh in range(2):
                d = 4 * y + 2 * xh + xl
                out_ref[d, 192:208, :] = jnp.concatenate([extra, extra], axis=0)
    for d in range(16):
        out_ref[d, :192, :] = out_ref[d, :192, :] * factor


def middle_taps(core, f, g, fx, gx):
    return pl.pallas_call(
        middle_kernel,
        out_shape=jax.ShapeDtypeStruct((16, 208, 128), f32),
        in_specs=[smem()] + [vmem()] * 4,
        out_specs=vmem(),
        scratch_shapes=[
            pltpu.VMEM((HALF, 1152), bf16),
            pltpu.VMEM((3, HALF, 2 * S), bf16),
            pltpu.VMEM((C, 2 * S), bf16),
        ],
        compiler_params=params(20),
        cost_estimate=pl.CostEstimate(flops=2 * 3 * C * HALF * 2 * S, bytes_accessed=5_000_000, transcendentals=0),
        name="middle_taps",
    )(core, f, g, fx, gx)


def outer_kernel(core_ref, f_ref, g_ref, before_ref, after_ref, fx_ref, gx_ref, halo_ref, out_ref, ext, win, cot):
    core = core_ref[0]
    mine = pl.multiple_of(core * HALF, HALF)
    masks = column_masks(HALF)
    groups = (2 * core, 2 * core + 1)
    cot[:, :S] = g_ref[...]
    cot[:, S:] = gx_ref[...]
    for seg in range(2):
        if seg == 0:
            cells = f_ref[pl.ds(mine, HALF), :]
            before = (before_ref[0, pl.ds(mine, HALF), :], before_ref[0, C:, :])
            after = (after_ref[0, pl.ds(mine, HALF), :], after_ref[0, C:, :])
        else:
            cells = fx_ref[pl.ds(mine, HALF), :]
            before = (halo_ref[0, pl.ds(mine, HALF), :], halo_ref[0, C:, :])
            after = (halo_ref[1, pl.ds(mine, HALF), :], halo_ref[1, C:, :])
        fill(ext, HALF, cells, before, after, groups)
        for a in range(2):
            for b in range(3):
                win[3 * a + b, :, S * seg:S * (seg + 1)] = window(ext, (0, HALF), 2 * a - 1, b - 1, masks)
    peak = jnp.zeros((16, 128), f32)
    for t in range(6):
        peak = store_tap(out_ref, contract(cot[...], win[t]), t, peak)
    power = power_of(peak)
    factor = jnp.exp2(power)
    for d in range(16):
        out_ref[d, :384, :] = out_ref[d, :384, :] * factor
        out_ref[d, 384:400, :] = jnp.broadcast_to(power, (16, 128))


def outer_taps(core, f, g, before, after, fx, gx, halo):
    return pl.pallas_call(
        outer_kernel,
        out_shape=jax.ShapeDtypeStruct((16, 400, 128), f32),
        in_specs=[smem()] + [vmem()] * 7,
        out_specs=vmem(),
        scratch_shapes=[
            pltpu.VMEM((HALF, 1152), bf16),
            pltpu.VMEM((6, HALF, 2 * S), bf16),
            pltpu.VMEM((C, 2 * S), bf16),
        ],
        compiler_params=params(24),
        cost_estimate=pl.CostEstimate(flops=2 * 6 * C * HALF * 2 * S, bytes_accessed=7_000_000, transcendentals=0),
        name="outer_taps",
    )(core, f, g, before, after, fx, gx, halo)


def load_kernel(place_ref, own_ref, other_refs, kern):
    core, low = place_ref[0], place_ref[1]
    for half, refs in ((core, (own_ref,)), (1 - core, other_refs)):
        size = HALF // len(refs)
        for t in range(TAPS):
            lanes = pl.ds(pl.multiple_of(t * C + half * HALF, HALF), HALF)
            for k in range(2):
                for j, ref in enumerate(refs):
                    first = HALF * (low if k == 0 else 1 - low) + j * size
                    kern[pl.ds(pl.multiple_of(first, size), size), lanes] = ref[:, k, t].reshape(size, HALF)


def forward_kernel(core_ref, f_ref, before_ref, after_ref, own_ref, o0_ref, o1_ref, o2_ref, o3_ref, bias_ref, out_ref, ext, win, kern):
    load_kernel(core_ref, own_ref, (o0_ref, o1_ref, o2_ref, o3_ref), kern)
    masks = column_masks(C)
    fill(ext, C, f_ref[...], (before_ref[0, :C, :], before_ref[0, C:, :]), (after_ref[0, :C, :], after_ref[0, C:, :]), GROUPS)
    for a in range(3):
        for b in range(3):
            t = 3 * a + b
            win[C * t:C * (t + 1), :] = window(ext, (0, C), a - 1, b - 1, masks)
    for m in range(2):
        rows = slice(HALF * m, HALF * (m + 1))
        total = jnp.dot(kern[rows, :], win[...], preferred_element_type=f32)
        out_ref[rows, :] = (total + bias_ref[rows, :]).astype(bf16)


def backward_kernel(core_ref, g_ref, before_ref, after_ref, own_ref, o0_ref, o1_ref, o2_ref, o3_ref, grad_ref, ext, win, kern):
    load_kernel(core_ref, own_ref, (o0_ref, o1_ref, o2_ref, o3_ref), kern)
    masks = column_masks(C)
    fill(ext, C, g_ref[...], (before_ref[1, :C, :], before_ref[1, C:, :]), (after_ref[1, :C, :], after_ref[1, C:, :]), GROUPS)
    for a in range(3):
        for b in range(3):
            t = 3 * a + b
            win[C * t:C * (t + 1), :] = window(ext, (0, C), 1 - a, 1 - b, masks)
    for m in range(2):
        total = jnp.zeros((HALF, S), f32)
        for t in range(TAPS):
            total = total + lax.dot_general(
                kern[:, C * t + HALF * m:C * t + HALF * (m + 1)],
                win[C * t:C * (t + 1), :],
                (((0,), (0,)), ((), ())),
                preferred_element_type=f32,
            )
        grad_ref[HALF * m:HALF * (m + 1), :] = total.astype(bf16)


def convolve(body, name, *args):
    return pl.pallas_call(
        body,
        out_shape=jax.ShapeDtypeStruct((C, S), bf16),
        in_specs=[smem()] + [vmem()] * (len(args) - 1),
        out_specs=vmem(),
        scratch_shapes=[
            pltpu.VMEM((C, 1152), bf16),
            pltpu.VMEM((TAPS * C, S), bf16),
            pltpu.VMEM((C, TAPS * C), bf16),
        ],
        compiler_params=params(32),
        cost_estimate=pl.CostEstimate(flops=1_000_000, bytes_accessed=1_000_000, transcendentals=0),
        name=name,
    )(*args)


def swap_cores(x):
    return lax.ppermute(x, "core", [(0, 1), (1, 0)])


def sum_sources(got, rows, power):
    factor = jnp.exp2(-power)[:, None, None]
    return jnp.sum(got[:, :rows].astype(f32) * factor, axis=0)


def after(values, *first):
    return lax.optimization_barrier((tuple(values), first))[0]


def local(frames, weight, bias, cotangent):
    f = frames.reshape(C, S)
    g = cotangent.reshape(C, S)
    core = lax.axis_index("core")
    place = jnp.stack((core, lax.axis_index("xl"))).astype(jnp.int32)
    up = [(i, i + 1) for i in range(63)]
    down = [(i + 1, i) for i in range(63)]
    plane = ("y", "xh", "xl")

    taps = weight.transpose(1, 2, 0, 3).reshape(TAPS, 32, C)
    half = lax.dynamic_slice_in_dim(taps, core * HALF, HALF, axis=2)
    beside = lax.ppermute(half, "xl", [(0, 1), (1, 0)])

    fx = swap_cores(f)
    gx = swap_cores(g)
    last, first = pack(f, g)
    half, beside = after((half, beside), last, fx, gx)
    own = lax.all_gather(jnp.stack((half, beside)), "z", axis=0, tiled=False)
    above = lax.ppermute(last, CELLS, up)
    below = lax.ppermute(first, CELLS, down)

    part = middle_taps(place, f, g, fx, gx)
    sent = part.astype(f16)
    got = lax.all_to_all(sent, plane, 0, 0, tiled=True)
    above, below = after((above, below), sent)
    halo = swap_cores(jnp.stack((above[0], below[0])))

    part2 = outer_taps(place, f, g, above, below, fx, gx, halo)
    (sent2,) = after((part2.astype(f16),), got)
    got2 = lax.all_to_all(sent2, plane, 0, 0, tiled=True)
    (own,) = after((own,), got)
    other = tuple(swap_cores(own[2 * k:2 * k + 2]) for k in range(4))
    outputs = convolve(forward_kernel, "forward", place, f, above, below, own, *other, bias.reshape(C, 1))
    got2, outputs = lax.optimization_barrier((got2, outputs))

    extra = lax.optimization_barrier(got[:, 192:200]).astype(f32)
    extra2 = lax.optimization_barrier(got2[:, 384:392]).astype(f32)
    middle = sum_sources(got, 192, extra[:, 0, 8]).reshape(3, 8, 8, 128)
    outer = sum_sources(got2, 384, extra2[:, 0, 8]).reshape(6, 8, 8, 128)
    ends = jnp.sum(extra * jnp.exp2(-extra[:, 0, 9])[:, None, None], axis=0)
    ends = jnp.broadcast_to(ends[:, :8].T[:, :, None], (8, 8, 128))[None]
    line = jnp.concatenate((outer[:3], middle, outer[3:], ends), axis=0).transpose(1, 0, 2, 3)
    lines = lax.all_to_all(line, "z", 0, 0, tiled=True)
    scale = 1.0 / math.sqrt(4 * 256 * 160)
    done = jnp.sum(lines, axis=0) * scale
    whole = jnp.broadcast_to(done, (16, 10, 8, 128))
    whole, g = lax.optimization_barrier((whole, g))
    whole = lax.all_to_all(whole, ("y", "xh", "core"), 0, 0, tiled=True)
    grad_frames = convolve(backward_kernel, "backward", place, g, above, below, own, *other)
    whole, grad_frames = lax.optimization_barrier((whole, grad_frames))
    whole = whole.reshape(4, 2, 2, 10, 8, 128)
    grad_weight = whole[:, :, :, :9].reshape(4, 2, 2, 3, 3, 8, 128)
    grad_weight = grad_weight.transpose(0, 5, 3, 4, 2, 1, 6).reshape(32, 3, 3, C)
    grad_bias = whole[:, 0, 0, 9, :, 0].reshape(32)
    return (outputs.reshape(C, 1, S), grad_frames.reshape(C, 1, S), grad_weight, grad_bias)


def solution(mesh):
    fine = Mesh(mesh.devices.reshape(SIZES), AXES)
    cells = P(None, "y", CELLS)
    rows = ("xl", "z")
    in_specs = (cells, P(rows, None, None, None), P(), cells)
    out_specs = (cells, cells, P(rows, None, None, None), P(rows))
    return jax.shard_map(local, mesh=fine, in_specs=in_specs, out_specs=out_specs, check_vma=False)
```

```python
import functools
import math

import jax
import jax.numpy as jnp
from jax import lax
from jax.experimental import pallas as pl
from jax.experimental.pallas import tpu as pltpu
from jax.sharding import Mesh, PartitionSpec as P

C = 512
HALF = 256
W = 160
S = 640
TAPS = 9
GROUPS = (0, 1, 2, 3)
AXES = ("y", "xh", "core", "xl", "z")
SIZES = (4, 2, 2, 2, 8)
CELLS = ("xh", "core", "xl", "z")

bf16 = jnp.bfloat16
f16 = jnp.float16
f32 = jnp.float32


def vmem():
    return pl.BlockSpec(memory_space=pltpu.VMEM)


def smem():
    return pl.BlockSpec(memory_space=pltpu.SMEM)


def params(mib):
    return pltpu.CompilerParams(vmem_limit_bytes=mib * 1024 * 1024)


def roll(x, shift):
    return pltpu.roll(x, shift % x.shape[-1], x.ndim - 1)


def pack_row(wide, tile, start):
    lane = lax.broadcasted_iota(jnp.int32, (128, 128), 1)
    tile = tile.astype(f32)
    total = jnp.zeros((128, 128), f32)
    for g in range(4):
        part = roll(tile[128 * g:128 * (g + 1)], 32 * g - start)
        total = jnp.where((lane >= 32 * g) & (lane < 32 * g + 32), part, total)
    return jnp.concatenate([wide, total.astype(bf16)], axis=0)


def pack_kernel(f_ref, g_ref, last_ref, first_ref):
    for k, x in enumerate((f_ref, g_ref)):
        last_ref[k] = pack_row(x[:, 512:640], x[:, 384:512], 96)
        first_ref[k] = pack_row(x[:, 0:128], x[:, 128:256], 0)


def pack(f, g):
    rows = jax.ShapeDtypeStruct((2, 640, 128), bf16)
    return pl.pallas_call(
        pack_kernel,
        out_shape=(rows, rows),
        in_specs=[vmem(), vmem()],
        out_specs=(vmem(), vmem()),
        compiler_params=params(12),
        name="pack",
    )(f, g)


def column_masks(rows):
    column = lax.broadcasted_iota(jnp.int32, (rows, S), 1) % W
    return column != 0, None, column != W - 1


def fill(ext, rows, cells, before, after, groups):
    ext[:rows, 256:896] = cells
    ext[:rows, 128:256] = before[0]
    ext[:rows, 896:1024] = after[0]
    tail_before = before[1].astype(f32)
    tail_after = after[1].astype(f32)
    for k, g in enumerate(groups):
        ext[128 * k:128 * (k + 1), 0:128] = pltpu.roll(tail_before, (96 - 32 * g) % 128, 1).astype(bf16)
        ext[128 * k:128 * (k + 1), 1024:1152] = pltpu.roll(tail_after, (128 - 32 * g) % 128, 1).astype(bf16)


def window(ext, rows, da, db, masks):
    start = 256 + da * W + db
    x = ext[pl.ds(rows[0], rows[1]), :][:, start:start + S]
    mask = masks[db + 1]
    if mask is not None:
        x = jnp.where(mask, x, jnp.zeros_like(x))
    return x


def pair_rows(part, y, xh, xl, k):
    lanes = slice(128 * xh, 128 * xh + 128)
    o = 256 * xl + 64 * k + 8 * y
    return jnp.concatenate([part[o:o + 8, lanes], part[o + 32:o + 40, lanes]], axis=0)


def store_tap(out_ref, part, position, peak):
    for y in range(4):
        for xh in range(2):
            for xl in range(2):
                for k in range(4):
                    block = pair_rows(part, y, xh, xl, k)
                    row = 64 * position + 16 * k
                    out_ref[4 * y + 2 * xh + xl, row:row + 16, :] = block
                    peak = jnp.maximum(peak, jnp.abs(block))
    return peak


def power_of(peak):
    top = jnp.max(jnp.max(peak, axis=1, keepdims=True), axis=0, keepdims=True)
    return 14.0 - jnp.floor(jnp.log2(jnp.maximum(top, 1e-30)))


def contract(cot, win):
    return lax.dot_general(cot, win, (((1,), (1,)), ((), ())), preferred_element_type=f32)


def middle_kernel(core_ref, f_ref, g_ref, fx_ref, gx_ref, out_ref, ext, win, cot):
    core = core_ref[0]
    mine = pl.multiple_of(core * HALF, HALF)
    masks = column_masks(HALF)
    cot[:, :S] = g_ref[...]
    cot[:, S:] = gx_ref[...]
    ext[...] = jnp.zeros_like(ext)
    for seg in range(2):
        ext[:, 256:896] = (f_ref, fx_ref)[seg][pl.ds(mine, HALF), :]
        for b in range(3):
            win[b, :, S * seg:S * (seg + 1)] = window(ext, (0, HALF), 0, b - 1, masks)
    peak = jnp.zeros((16, 128), f32)
    for b in range(3):
        peak = store_tap(out_ref, contract(cot[...], win[b]), b, peak)
    power = power_of(peak)
    factor = jnp.exp2(power)
    total = jnp.zeros((C, 128), f32)
    for k in range(2 * S // 128):
        total = total + cot[:, 128 * k:128 * (k + 1)].astype(f32)
    total = jnp.sum(total, axis=1, keepdims=True)
    bias_power = power_of(jnp.abs(total))
    total = jnp.broadcast_to(total * jnp.exp2(bias_power), (C, 128))
    lane = lax.broadcasted_iota(jnp.int32, (8, 128), 1)
    for y in range(4):
        for xl in range(2):
            extra = jnp.where(lane == 8, jnp.broadcast_to(power, (8, 128)), jnp.broadcast_to(bias_power, (8, 128)))
            for z in range(8):
                o = 256 * xl + 32 * z + 8 * y
                extra = jnp.where(lane == z, total[o:o + 8, :], extra)
            for xh in range(2):
                d = 4 * y + 2 * xh + xl
                out_ref[d, 192:208, :] = jnp.concatenate([extra, extra], axis=0)
    for d in range(16):
        out_ref[d, :192, :] = out_ref[d, :192, :] * factor


def middle_taps(core, f, g, fx, gx):
    return pl.pallas_call(
        middle_kernel,
        out_shape=jax.ShapeDtypeStruct((16, 208, 128), f32),
        in_specs=[smem()] + [vmem()] * 4,
        out_specs=vmem(),
        scratch_shapes=[
            pltpu.VMEM((HALF, 1152), bf16),
            pltpu.VMEM((3, HALF, 2 * S), bf16),
            pltpu.VMEM((C, 2 * S), bf16),
        ],
        compiler_params=params(20),
        cost_estimate=pl.CostEstimate(flops=2 * 3 * C * HALF * 2 * S, bytes_accessed=5_000_000, transcendentals=0),
        name="middle_taps",
    )(core, f, g, fx, gx)


def outer_kernel(core_ref, f_ref, g_ref, before_ref, after_ref, fx_ref, gx_ref, halo_ref, out_ref, ext, win, cot):
    core = core_ref[0]
    mine = pl.multiple_of(core * HALF, HALF)
    masks = column_masks(HALF)
    groups = (2 * core, 2 * core + 1)
    cot[:, :S] = g_ref[...]
    cot[:, S:] = gx_ref[...]
    for seg in range(2):
        if seg == 0:
            cells = f_ref[pl.ds(mine, HALF), :]
            before = (before_ref[0, pl.ds(mine, HALF), :], before_ref[0, C:, :])
            after = (after_ref[0, pl.ds(mine, HALF), :], after_ref[0, C:, :])
        else:
            cells = fx_ref[pl.ds(mine, HALF), :]
            before = (halo_ref[0, pl.ds(mine, HALF), :], halo_ref[0, C:, :])
            after = (halo_ref[1, pl.ds(mine, HALF), :], halo_ref[1, C:, :])
        fill(ext, HALF, cells, before, after, groups)
        for a in range(2):
            for b in range(3):
                win[3 * a + b, :, S * seg:S * (seg + 1)] = window(ext, (0, HALF), 2 * a - 1, b - 1, masks)
    peak = jnp.zeros((16, 128), f32)
    for t in range(6):
        peak = store_tap(out_ref, contract(cot[...], win[t]), t, peak)
    power = power_of(peak)
    factor = jnp.exp2(power)
    for d in range(16):
        out_ref[d, :384, :] = out_ref[d, :384, :] * factor
        out_ref[d, 384:400, :] = jnp.broadcast_to(power, (16, 128))


def outer_taps(core, f, g, before, after, fx, gx, halo):
    return pl.pallas_call(
        outer_kernel,
        out_shape=jax.ShapeDtypeStruct((16, 400, 128), f32),
        in_specs=[smem()] + [vmem()] * 7,
        out_specs=vmem(),
        scratch_shapes=[
            pltpu.VMEM((HALF, 1152), bf16),
            pltpu.VMEM((6, HALF, 2 * S), bf16),
            pltpu.VMEM((C, 2 * S), bf16),
        ],
        compiler_params=params(24),
        cost_estimate=pl.CostEstimate(flops=2 * 6 * C * HALF * 2 * S, bytes_accessed=7_000_000, transcendentals=0),
        name="outer_taps",
    )(core, f, g, before, after, fx, gx, halo)


def load_kernel(place_ref, own_ref, other_refs, kern):
    core, low = place_ref[0], place_ref[1]
    for half, refs in ((core, (own_ref,)), (1 - core, other_refs)):
        size = HALF // len(refs)
        for t in range(TAPS):
            lanes = pl.ds(pl.multiple_of(t * C + half * HALF, HALF), HALF)
            for k in range(2):
                for j, ref in enumerate(refs):
                    first = HALF * (low if k == 0 else 1 - low) + j * size
                    kern[pl.ds(pl.multiple_of(first, size), size), lanes] = ref[:, k, t].reshape(size, HALF)


def forward_kernel(core_ref, f_ref, before_ref, after_ref, own_ref, o0_ref, o1_ref, o2_ref, o3_ref, bias_ref, out_ref, ext, win, kern):
    load_kernel(core_ref, own_ref, (o0_ref, o1_ref, o2_ref, o3_ref), kern)
    masks = column_masks(C)
    fill(ext, C, f_ref[...], (before_ref[0, :C, :], before_ref[0, C:, :]), (after_ref[0, :C, :], after_ref[0, C:, :]), GROUPS)
    for a in range(3):
        for b in range(3):
            t = 3 * a + b
            win[C * t:C * (t + 1), :] = window(ext, (0, C), a - 1, b - 1, masks)
    for m in range(2):
        rows = slice(HALF * m, HALF * (m + 1))
        total = jnp.dot(kern[rows, :], win[...], preferred_element_type=f32)
        out_ref[rows, :] = (total + bias_ref[rows, :]).astype(bf16)


def backward_kernel(core_ref, g_ref, before_ref, after_ref, own_ref, o0_ref, o1_ref, o2_ref, o3_ref, grad_ref, ext, win, kern):
    load_kernel(core_ref, own_ref, (o0_ref, o1_ref, o2_ref, o3_ref), kern)
    masks = column_masks(C)
    fill(ext, C, g_ref[...], (before_ref[1, :C, :], before_ref[1, C:, :]), (after_ref[1, :C, :], after_ref[1, C:, :]), GROUPS)
    for a in range(3):
        for b in range(3):
            t = 3 * a + b
            win[C * t:C * (t + 1), :] = window(ext, (0, C), 1 - a, 1 - b, masks)
    for m in range(2):
        total = jnp.zeros((HALF, S), f32)
        for t in range(TAPS):
            total = total + lax.dot_general(
                kern[:, C * t + HALF * m:C * t + HALF * (m + 1)],
                win[C * t:C * (t + 1), :],
                (((0,), (0,)), ((), ())),
                preferred_element_type=f32,
            )
        grad_ref[HALF * m:HALF * (m + 1), :] = total.astype(bf16)


def convolve(body, name, *args):
    return pl.pallas_call(
        body,
        out_shape=jax.ShapeDtypeStruct((C, S), bf16),
        in_specs=[smem()] + [vmem()] * (len(args) - 1),
        out_specs=vmem(),
        scratch_shapes=[
            pltpu.VMEM((C, 1152), bf16),
            pltpu.VMEM((TAPS * C, S), bf16),
            pltpu.VMEM((C, TAPS * C), bf16),
        ],
        compiler_params=params(32),
        cost_estimate=pl.CostEstimate(flops=2 * TAPS * C * C * S, bytes_accessed=7_000_000, transcendentals=0),
        name=name,
    )(*args)


def swap_cores(x):
    return lax.ppermute(x, "core", [(0, 1), (1, 0)])


def sum_sources(got, rows, power):
    factor = jnp.exp2(-power)[:, None, None]
    return jnp.sum(got[:, :rows].astype(f32) * factor, axis=0)


def after(values, *first):
    return lax.optimization_barrier((tuple(values), first))[0]


def local(frames, weight, bias, cotangent):
    f = frames.reshape(C, S)
    g = cotangent.reshape(C, S)
    core = lax.axis_index("core")
    place = jnp.stack((core, lax.axis_index("xl"))).astype(jnp.int32)
    up = [(i, i + 1) for i in range(63)]
    down = [(i + 1, i) for i in range(63)]
    plane = ("y", "xh", "xl")

    taps = weight.transpose(1, 2, 0, 3).reshape(TAPS, 32, C)
    half = lax.dynamic_slice_in_dim(taps, core * HALF, HALF, axis=2)
    beside = lax.ppermute(half, "xl", [(0, 1), (1, 0)])

    fx = swap_cores(f)
    gx = swap_cores(g)
    last, first = pack(f, g)
    half, beside = after((half, beside), last, fx, gx)
    own = lax.all_gather(jnp.stack((half, beside)), "z", axis=0, tiled=False)
    above = lax.ppermute(last, CELLS, up)
    below = lax.ppermute(first, CELLS, down)

    part = middle_taps(place, f, g, fx, gx)
    sent = part.astype(f16)
    got = lax.all_to_all(sent, plane, 0, 0, tiled=True)
    above, below = after((above, below), sent)
    halo = swap_cores(jnp.stack((above[0], below[0])))

    part2 = outer_taps(place, f, g, above, below, fx, gx, halo)
    (sent2,) = after((part2.astype(f16),), got)
    got2 = lax.all_to_all(sent2, plane, 0, 0, tiled=True)
    (own,) = after((own,), got)
    other = tuple(swap_cores(own[2 * k:2 * k + 2]) for k in range(4))
    outputs = convolve(forward_kernel, "forward", place, f, above, below, own, *other, bias.reshape(C, 1))
    got2, outputs = lax.optimization_barrier((got2, outputs))

    extra = lax.optimization_barrier(got[:, 192:200]).astype(f32)
    extra2 = lax.optimization_barrier(got2[:, 384:392]).astype(f32)
    middle = sum_sources(got, 192, extra[:, 0, 8]).reshape(3, 8, 8, 128)
    outer = sum_sources(got2, 384, extra2[:, 0, 8]).reshape(6, 8, 8, 128)
    ends = jnp.sum(extra * jnp.exp2(-extra[:, 0, 9])[:, None, None], axis=0)
    ends = jnp.broadcast_to(ends[:, :8].T[:, :, None], (8, 8, 128))[None]
    line = jnp.concatenate((outer[:3], middle, outer[3:], ends), axis=0).transpose(1, 0, 2, 3)
    lines = lax.all_to_all(line, "z", 0, 0, tiled=True)
    (g,) = after((g,), line)
    grad_frames = convolve(backward_kernel, "backward", place, g, above, below, own, *other)
    lines, grad_frames = lax.optimization_barrier((lines, grad_frames))
    scale = 1.0 / math.sqrt(4 * 256 * 160)
    done = jnp.sum(lines, axis=0) * scale
    whole = jnp.broadcast_to(done, (16, 10, 8, 128))
    whole = lax.all_to_all(whole, ("y", "xh", "core"), 0, 0, tiled=True)
    whole = whole.reshape(4, 2, 2, 10, 8, 128)
    grad_weight = whole[:, :, :, :9].reshape(4, 2, 2, 3, 3, 8, 128)
    grad_weight = grad_weight.transpose(0, 5, 3, 4, 2, 1, 6).reshape(32, 3, 3, C)
    grad_bias = whole[:, 0, 0, 9, :, 0].reshape(32)
    return (outputs.reshape(C, 1, S), grad_frames.reshape(C, 1, S), grad_weight, grad_bias)


def solution(mesh):
    fine = Mesh(mesh.devices.reshape(SIZES), AXES)
    cells = P(None, "y", CELLS)
    rows = ("xl", "z")
    in_specs = (cells, P(rows, None, None, None), P(), cells)
    out_specs = (cells, cells, P(rows, None, None, None), P(rows))
    return jax.shard_map(local, mesh=fine, in_specs=in_specs, out_specs=out_specs, check_vma=False)
```

```python
import functools
import math

import jax
import jax.numpy as jnp
from jax import lax
from jax.experimental import pallas as pl
from jax.experimental.pallas import tpu as pltpu
from jax.sharding import Mesh, PartitionSpec as P

C = 512
HALF = 256
W = 160
S = 640
TAPS = 9
GROUPS = (0, 1, 2, 3)
AXES = ("y", "xh", "core", "xl", "z")
SIZES = (4, 2, 2, 2, 8)
CELLS = ("xh", "core", "xl", "z")

bf16 = jnp.bfloat16
f16 = jnp.float16
f32 = jnp.float32


def vmem():
    return pl.BlockSpec(memory_space=pltpu.VMEM)


def smem():
    return pl.BlockSpec(memory_space=pltpu.SMEM)


def params(mib):
    return pltpu.CompilerParams(vmem_limit_bytes=mib * 1024 * 1024)


def roll(x, shift):
    return pltpu.roll(x, shift % x.shape[-1], x.ndim - 1)


def pack_row(wide, tile, start):
    lane = lax.broadcasted_iota(jnp.int32, (128, 128), 1)
    tile = tile.astype(f32)
    total = jnp.zeros((128, 128), f32)
    for g in range(4):
        part = roll(tile[128 * g:128 * (g + 1)], 32 * g - start)
        total = jnp.where((lane >= 32 * g) & (lane < 32 * g + 32), part, total)
    return jnp.concatenate([wide, total.astype(bf16)], axis=0)


def pack_kernel(f_ref, g_ref, fl_ref, ff_ref, gl_ref, gf_ref):
    for x, last, first in ((f_ref, fl_ref, ff_ref), (g_ref, gl_ref, gf_ref)):
        last[...] = pack_row(x[:, 512:640], x[:, 384:512], 96)
        first[...] = pack_row(x[:, 0:128], x[:, 128:256], 0)


def pack(f, g):
    row = jax.ShapeDtypeStruct((640, 128), bf16)
    return pl.pallas_call(
        pack_kernel,
        out_shape=(row,) * 4,
        in_specs=[vmem(), vmem()],
        out_specs=(vmem(),) * 4,
        compiler_params=params(12),
        name="pack",
    )(f, g)


def column_masks(rows):
    column = lax.broadcasted_iota(jnp.int32, (rows, S), 1) % W
    return column != 0, None, column != W - 1


def fill(ext, rows, cells, before, after, groups):
    ext[:rows, 256:896] = cells
    ext[:rows, 128:256] = before[0]
    ext[:rows, 896:1024] = after[0]
    tail_before = before[1].astype(f32)
    tail_after = after[1].astype(f32)
    for k, g in enumerate(groups):
        ext[128 * k:128 * (k + 1), 0:128] = pltpu.roll(tail_before, (96 - 32 * g) % 128, 1).astype(bf16)
        ext[128 * k:128 * (k + 1), 1024:1152] = pltpu.roll(tail_after, (128 - 32 * g) % 128, 1).astype(bf16)


def window(ext, rows, da, db, masks):
    start = 256 + da * W + db
    x = ext[pl.ds(rows[0], rows[1]), :][:, start:start + S]
    mask = masks[db + 1]
    if mask is not None:
        x = jnp.where(mask, x, jnp.zeros_like(x))
    return x


def pair_rows(part, y, xh, xl, k):
    lanes = slice(128 * xh, 128 * xh + 128)
    o = 256 * xl + 64 * k + 8 * y
    return jnp.concatenate([part[o:o + 8, lanes], part[o + 32:o + 40, lanes]], axis=0)


def store_tap(out_ref, part, position, peak):
    for y in range(4):
        for xh in range(2):
            for xl in range(2):
                for k in range(4):
                    block = pair_rows(part, y, xh, xl, k)
                    row = 64 * position + 16 * k
                    out_ref[4 * y + 2 * xh + xl, row:row + 16, :] = block
                    peak = jnp.maximum(peak, jnp.abs(block))
    return peak


def power_of(peak):
    top = jnp.max(jnp.max(peak, axis=1, keepdims=True), axis=0, keepdims=True)
    return 14.0 - jnp.floor(jnp.log2(jnp.maximum(top, 1e-30)))


def contract(cot, win):
    return lax.dot_general(cot, win, (((1,), (1,)), ((), ())), preferred_element_type=f32)


def middle_kernel(core_ref, f_ref, g_ref, fx_ref, gx_ref, out_ref, ext, win, cot):
    core = core_ref[0]
    mine = pl.multiple_of(core * HALF, HALF)
    masks = column_masks(HALF)
    cot[:, :S] = g_ref[...]
    cot[:, S:] = gx_ref[...]
    ext[...] = jnp.zeros_like(ext)
    for seg in range(2):
        ext[:, 256:896] = (f_ref, fx_ref)[seg][pl.ds(mine, HALF), :]
        for b in range(3):
            win[b, :, S * seg:S * (seg + 1)] = window(ext, (0, HALF), 0, b - 1, masks)
    peak = jnp.zeros((16, 128), f32)
    for b in range(3):
        peak = store_tap(out_ref, contract(cot[...], win[b]), b, peak)
    power = power_of(peak)
    factor = jnp.exp2(power)
    total = jnp.zeros((C, 128), f32)
    for k in range(2 * S // 128):
        total = total + cot[:, 128 * k:128 * (k + 1)].astype(f32)
    total = jnp.sum(total, axis=1, keepdims=True)
    bias_power = power_of(jnp.abs(total))
    total = jnp.broadcast_to(total * jnp.exp2(bias_power), (C, 128))
    lane = lax.broadcasted_iota(jnp.int32, (8, 128), 1)
    for y in range(4):
        for xl in range(2):
            extra = jnp.where(lane == 8, jnp.broadcast_to(power, (8, 128)), jnp.broadcast_to(bias_power, (8, 128)))
            for z in range(8):
                o = 256 * xl + 32 * z + 8 * y
                extra = jnp.where(lane == z, total[o:o + 8, :], extra)
            for xh in range(2):
                d = 4 * y + 2 * xh + xl
                out_ref[d, 192:208, :] = jnp.concatenate([extra, extra], axis=0)
    for d in range(16):
        out_ref[d, :192, :] = out_ref[d, :192, :] * factor


def middle_taps(core, f, g, fx, gx):
    return pl.pallas_call(
        middle_kernel,
        out_shape=jax.ShapeDtypeStruct((16, 208, 128), f32),
        in_specs=[smem()] + [vmem()] * 4,
        out_specs=vmem(),
        scratch_shapes=[
            pltpu.VMEM((HALF, 1152), bf16),
            pltpu.VMEM((3, HALF, 2 * S), bf16),
            pltpu.VMEM((C, 2 * S), bf16),
        ],
        compiler_params=params(20),
        cost_estimate=pl.CostEstimate(flops=2 * 3 * C * HALF * 2 * S, bytes_accessed=5_000_000, transcendentals=0),
        name="middle_taps",
    )(core, f, g, fx, gx)


def outer_kernel(core_ref, f_ref, g_ref, before_ref, after_ref, fx_ref, gx_ref, halo_ref, out_ref, ext, win, cot):
    core = core_ref[0]
    mine = pl.multiple_of(core * HALF, HALF)
    masks = column_masks(HALF)
    groups = (2 * core, 2 * core + 1)
    cot[:, :S] = g_ref[...]
    cot[:, S:] = gx_ref[...]
    for seg in range(2):
        if seg == 0:
            cells = f_ref[pl.ds(mine, HALF), :]
            before = (before_ref[pl.ds(mine, HALF), :], before_ref[C:, :])
            after = (after_ref[pl.ds(mine, HALF), :], after_ref[C:, :])
        else:
            cells = fx_ref[pl.ds(mine, HALF), :]
            before = (halo_ref[0, pl.ds(mine, HALF), :], halo_ref[0, C:, :])
            after = (halo_ref[1, pl.ds(mine, HALF), :], halo_ref[1, C:, :])
        fill(ext, HALF, cells, before, after, groups)
        for a in range(2):
            for b in range(3):
                win[3 * a + b, :, S * seg:S * (seg + 1)] = window(ext, (0, HALF), 2 * a - 1, b - 1, masks)
    peak = jnp.zeros((16, 128), f32)
    for t in range(6):
        peak = store_tap(out_ref, contract(cot[...], win[t]), t, peak)
    power = power_of(peak)
    factor = jnp.exp2(power)
    for d in range(16):
        out_ref[d, :384, :] = out_ref[d, :384, :] * factor
        out_ref[d, 384:400, :] = jnp.broadcast_to(power, (16, 128))


def outer_taps(core, f, g, before, after, fx, gx, halo):
    return pl.pallas_call(
        outer_kernel,
        out_shape=jax.ShapeDtypeStruct((16, 400, 128), f32),
        in_specs=[smem()] + [vmem()] * 7,
        out_specs=vmem(),
        scratch_shapes=[
            pltpu.VMEM((HALF, 1152), bf16),
            pltpu.VMEM((6, HALF, 2 * S), bf16),
            pltpu.VMEM((C, 2 * S), bf16),
        ],
        compiler_params=params(24),
        cost_estimate=pl.CostEstimate(flops=2 * 6 * C * HALF * 2 * S, bytes_accessed=7_000_000, transcendentals=0),
        name="outer_taps",
    )(core, f, g, before, after, fx, gx, halo)


def load_kernel(place_ref, own_ref, other_refs, kern):
    core, low = place_ref[0], place_ref[1]
    for half, refs in ((core, (own_ref,)), (1 - core, other_refs)):
        size = HALF // len(refs)
        for t in range(TAPS):
            lanes = pl.ds(pl.multiple_of(t * C + half * HALF, HALF), HALF)
            for k in range(2):
                for j, ref in enumerate(refs):
                    first = HALF * (low if k == 0 else 1 - low) + j * size
                    kern[pl.ds(pl.multiple_of(first, size), size), lanes] = ref[:, k, t].reshape(size, HALF)


def forward_kernel(core_ref, f_ref, before_ref, after_ref, own_ref, o0_ref, o1_ref, o2_ref, o3_ref, bias_ref, out_ref, ext, win, kern):
    load_kernel(core_ref, own_ref, (o0_ref, o1_ref, o2_ref, o3_ref), kern)
    masks = column_masks(C)
    fill(ext, C, f_ref[...], (before_ref[:C, :], before_ref[C:, :]), (after_ref[:C, :], after_ref[C:, :]), GROUPS)
    for a in range(3):
        for b in range(3):
            t = 3 * a + b
            win[C * t:C * (t + 1), :] = window(ext, (0, C), a - 1, b - 1, masks)
    for m in range(2):
        rows = slice(HALF * m, HALF * (m + 1))
        total = jnp.dot(kern[rows, :], win[...], preferred_element_type=f32)
        out_ref[rows, :] = (total + bias_ref[rows, :]).astype(bf16)


def backward_kernel(core_ref, g_ref, before_ref, after_ref, own_ref, o0_ref, o1_ref, o2_ref, o3_ref, grad_ref, ext, win, kern):
    load_kernel(core_ref, own_ref, (o0_ref, o1_ref, o2_ref, o3_ref), kern)
    masks = column_masks(C)
    fill(ext, C, g_ref[...], (before_ref[:C, :], before_ref[C:, :]), (after_ref[:C, :], after_ref[C:, :]), GROUPS)
    for a in range(3):
        for b in range(3):
            t = 3 * a + b
            win[C * t:C * (t + 1), :] = window(ext, (0, C), 1 - a, 1 - b, masks)
    for m in range(2):
        total = jnp.zeros((HALF, S), f32)
        for t in range(TAPS):
            total = total + lax.dot_general(
                kern[:, C * t + HALF * m:C * t + HALF * (m + 1)],
                win[C * t:C * (t + 1), :],
                (((0,), (0,)), ((), ())),
                preferred_element_type=f32,
            )
        grad_ref[HALF * m:HALF * (m + 1), :] = total.astype(bf16)


def convolve(body, name, *args):
    return pl.pallas_call(
        body,
        out_shape=jax.ShapeDtypeStruct((C, S), bf16),
        in_specs=[smem()] + [vmem()] * (len(args) - 1),
        out_specs=vmem(),
        scratch_shapes=[
            pltpu.VMEM((C, 1152), bf16),
            pltpu.VMEM((TAPS * C, S), bf16),
            pltpu.VMEM((C, TAPS * C), bf16),
        ],
        compiler_params=params(32),
        cost_estimate=pl.CostEstimate(flops=2 * TAPS * C * C * S, bytes_accessed=7_000_000, transcendentals=0),
        name=name,
    )(*args)


def swap_cores(x):
    return lax.ppermute(x, "core", [(0, 1), (1, 0)])


def sum_sources(got, rows, power):
    factor = jnp.exp2(-power)[:, None, None]
    return jnp.sum(got[:, :rows].astype(f32) * factor, axis=0)


def after(values, *first):
    return lax.optimization_barrier((tuple(values), first))[0]


def local(frames, weight, bias, cotangent):
    f = frames.reshape(C, S)
    g = cotangent.reshape(C, S)
    core = lax.axis_index("core")
    place = jnp.stack((core, lax.axis_index("xl"))).astype(jnp.int32)
    up = [(i, i + 1) for i in range(63)]
    down = [(i + 1, i) for i in range(63)]
    plane = ("y", "xh", "xl")

    taps = weight.transpose(1, 2, 0, 3).reshape(TAPS, 32, C)
    half = lax.dynamic_slice_in_dim(taps, core * HALF, HALF, axis=2)
    beside = lax.ppermute(half, "xl", [(0, 1), (1, 0)])

    fx = swap_cores(f)
    gx = swap_cores(g)
    fl, ff, gl, gf = pack(f, g)
    half, beside = after((half, beside), fl, fx, gx)
    own = lax.all_gather(jnp.stack((half, beside)), "z", axis=0, tiled=False)
    above = lax.ppermute(fl, CELLS, up)
    below = lax.ppermute(ff, CELLS, down)

    part = middle_taps(place, f, g, fx, gx)
    sent = part.astype(f16)
    got = lax.all_to_all(sent, plane, 0, 0, tiled=True)
    above, below = after((above, below), sent)
    halo = swap_cores(jnp.stack((above, below)))

    part2 = outer_taps(place, f, g, above, below, fx, gx, halo)
    (sent2,) = after((part2.astype(f16),), got)
    got2 = lax.all_to_all(sent2, plane, 0, 0, tiled=True)
    (own,) = after((own,), got)
    other = tuple(swap_cores(own[2 * k:2 * k + 2]) for k in range(4))
    outputs = convolve(forward_kernel, "forward", place, f, above, below, own, *other, bias.reshape(C, 1))
    gl, gf = after((gl, gf), *other)
    above_g = lax.ppermute(gl, CELLS, up)
    below_g = lax.ppermute(gf, CELLS, down)
    got2, outputs, above_g, below_g = lax.optimization_barrier((got2, outputs, above_g, below_g))

    extra = lax.optimization_barrier(got[:, 192:200]).astype(f32)
    extra2 = lax.optimization_barrier(got2[:, 384:392]).astype(f32)
    middle = sum_sources(got, 192, extra[:, 0, 8]).reshape(3, 8, 8, 128)
    outer = sum_sources(got2, 384, extra2[:, 0, 8]).reshape(6, 8, 8, 128)
    ends = jnp.sum(extra * jnp.exp2(-extra[:, 0, 9])[:, None, None], axis=0)
    ends = jnp.broadcast_to(ends[:, :8].T[:, :, None], (8, 8, 128))[None]
    line = jnp.concatenate((outer[:3], middle, outer[3:], ends), axis=0).transpose(1, 0, 2, 3)
    lines = lax.all_to_all(line, "z", 0, 0, tiled=True)
    (g,) = after((g,), line)
    grad_frames = convolve(backward_kernel, "backward", place, g, above_g, below_g, own, *other)
    lines, grad_frames = lax.optimization_barrier((lines, grad_frames))
    scale = 1.0 / math.sqrt(4 * 256 * 160)
    done = jnp.sum(lines, axis=0) * scale
    whole = jnp.broadcast_to(done, (16, 10, 8, 128))
    whole = lax.all_to_all(whole, ("y", "xh", "core"), 0, 0, tiled=True)
    whole = whole.reshape(4, 2, 2, 10, 8, 128)
    grad_weight = whole[:, :, :, :9].reshape(4, 2, 2, 3, 3, 8, 128)
    grad_weight = grad_weight.transpose(0, 5, 3, 4, 2, 1, 6).reshape(32, 3, 3, C)
    grad_bias = whole[:, 0, 0, 9, :, 0].reshape(32)
    return (outputs.reshape(C, 1, S), grad_frames.reshape(C, 1, S), grad_weight, grad_bias)


def solution(mesh):
    fine = Mesh(mesh.devices.reshape(SIZES), AXES)
    cells = P(None, "y", CELLS)
    rows = ("xl", "z")
    in_specs = (cells, P(rows, None, None, None), P(), cells)
    out_specs = (cells, cells, P(rows, None, None, None), P(rows))
    return jax.shard_map(local, mesh=fine, in_specs=in_specs, out_specs=out_specs, check_vma=False)
```
